32 devices in a mesh: fsdp: 2 (over x), ctx: 4 (over z), head: 4 (over y, core).
Axes of the slice: x: 2, y: 2, z: 4, core: 2. Of those that a mesh axis runs over, the one named last changes fastest.
Arguments:
- tokens: bfloat16 [4096, 2304], P(('fsdp', 'ctx', 'head')), may hold values from -6 to 6
- positions: int32 [4096], P('fsdp'), may hold values from 0 to 2047, as said below
- cotangent: bfloat16 [4096, 2304], P(('fsdp', 'ctx', 'head')), may hold values from -6 to 6
- qkv_weight: float32 [2304, 4096], P(('fsdp', 'ctx', 'head')), may hold values from -0.125 to 0.125
- qkv_first: float32 [2304, 4096], P(('fsdp', 'ctx', 'head'))
- qkv_second: float32 [2304, 4096], P(('fsdp', 'ctx', 'head')), as said below
- out_weight: float32 [2048, 2304], P(('fsdp', 'ctx', 'head')), may hold values from -0.125 to 0.125
- out_first: float32 [2048, 2304], P(('fsdp', 'ctx', 'head'))
- out_second: float32 [2048, 2304], P(('fsdp', 'ctx', 'head')), as said below
- gate_up: float32 [2, 2304, 9216], P(None, ('fsdp', 'ctx'), 'head'), may hold values from -0.125 to 0.125
- gate_up_first: float32 [2, 2304, 9216], P(None, ('fsdp', 'ctx'), 'head')
- gate_up_second: float32 [2, 2304, 9216], P(None, ('fsdp', 'ctx'), 'head'), as said below
- down_weight: float32 [9216, 2304], P('head', ('fsdp', 'ctx')), may hold values from -0.0625 to 0.0625
- down_first: float32 [9216, 2304], P('head', ('fsdp', 'ctx'))
- down_second: float32 [9216, 2304], P('head', ('fsdp', 'ctx')), as said below
- gains: float32 [2304, 4], P(('fsdp', 'ctx', 'head')), may hold values from -0.6 to 0.6
- gains_first: float32 [2304, 4], P(('fsdp', 'ctx', 'head'))
- gains_second: float32 [2304, 4], P(('fsdp', 'ctx', 'head')), as said below
Outputs:
- mixed_out: bfloat16 [4096, 2304], P(('fsdp', 'ctx', 'head'))
- tokens_grad: bfloat16 [4096, 2304], P(('fsdp', 'ctx', 'head'))
- qkv_grad: float32 [2304, 4096], P(('fsdp', 'ctx', 'head'))
- qkv_first_new: float32 [2304, 4096], P(('fsdp', 'ctx', 'head'))
- qkv_second_new: float32 [2304, 4096], P(('fsdp', 'ctx', 'head'))
- qkv_new: float32 [2304, 4096], P(('fsdp', 'ctx', 'head'))
- out_grad: float32 [2048, 2304], P(('fsdp', 'ctx', 'head'))
- out_first_new: float32 [2048, 2304], P(('fsdp', 'ctx', 'head'))
- out_second_new: float32 [2048, 2304], P(('fsdp', 'ctx', 'head'))
- out_new: float32 [2048, 2304], P(('fsdp', 'ctx', 'head'))
- gate_up_grad: float32 [2, 2304, 9216], P(None, ('fsdp', 'ctx'), 'head')
- gate_up_first_new: float32 [2, 2304, 9216], P(None, ('fsdp', 'ctx'), 'head')
- gate_up_second_new: float32 [2, 2304, 9216], P(None, ('fsdp', 'ctx'), 'head')
- gate_up_new: float32 [2, 2304, 9216], P(None, ('fsdp', 'ctx'), 'head')
- down_grad: float32 [9216, 2304], P('head', ('fsdp', 'ctx'))
- down_first_new: float32 [9216, 2304], P('head', ('fsdp', 'ctx'))
- down_second_new: float32 [9216, 2304], P('head', ('fsdp', 'ctx'))
- down_new: float32 [9216, 2304], P('head', ('fsdp', 'ctx'))
- gains_grad: float32 [2304, 4], P(('fsdp', 'ctx', 'head'))
- gains_first_new: float32 [2304, 4], P(('fsdp', 'ctx', 'head'))
- gains_second_new: float32 [2304, 4], P(('fsdp', 'ctx', 'head'))
- gains_new: float32 [2304, 4], P(('fsdp', 'ctx', 'head'))
The draws below stay inside these ranges and needn't reach their ends.
Inputs may be any that keep to these rules, and one draw needn't show every extreme that they name: Rows s * 2048 to (s + 1) * 2048 - 1 are sequence s and hold each position 0 to 2047 once; each aligned block of 512 rows holds either one run of consecutive rising positions or two such runs of 256. `qkv_second`: positive. `out_second`: positive. `gate_up_second`: positive. `down_second`: positive. `gains_second`: positive.
All inputs are finite; a program needn't handle non-finite values.
Results may differ from the reference program's by a relative error of at most 0.023.
Values may be sent and summed in bfloat16 or wider, within the bound.
No kernel may reach another device: no remote copies, remote signals or barrier semaphores. Data moves between devices by JAX's collectives and lax.ppermute only.
A program may use at most 384 MiB of HBM per device.

```python
import math
import jax
import jax.numpy as jnp
from jax import lax

D = 2304
QH = 8
KVH = 4
HD = 256
FF = 9216
STEP = 10
CTX_BLOCK = 512
SEQ = 2048
TOKENS = 4096
N_HEAD = 4


def first_moment(key, array_shape, factor):
    return factor * math.sqrt(TOKENS) / 9.0 * jax.random.normal(key, array_shape, jnp.float32)


def second_moment(key, array_shape, factor):
    spread = jnp.exp(jax.random.uniform(key, array_shape, jnp.float32, 0.0, math.log(4.0)))
    return factor * factor * TOKENS / 19.0 * spread


def draw_positions(key, part):
    key = jax.random.fold_in(key, 11)
    block_total = SEQ // CTX_BLOCK
    half_block = CTX_BLOCK // 2
    offsets = jnp.arange(CTX_BLOCK, dtype=jnp.int32)[None, :]
    pieces = []
    for sequence in range(TOKENS // SEQ):
        seq_key = jax.random.fold_in(key, sequence)
        order_key, mode_key = jax.random.split(seq_key)
        logical = jax.random.permutation(order_key, block_total).astype(jnp.int32)[:, None]
        paired_runs = jnp.where(offsets < half_block, logical * half_block + offsets, (2 * block_total - 1 - logical) * half_block + offsets - half_block)
        straight = logical * CTX_BLOCK + offsets
        use_paired = jax.random.randint(mode_key, (), 0, 2)
        pieces.append(jnp.where(use_paired == 1, paired_runs, straight).reshape(-1))
    return jnp.concatenate(pieces).astype(jnp.int32)


def draw_qkv_first(key, part):
    key = jax.random.fold_in(key, 31)
    return first_moment(key, (D, (QH + 2 * KVH) * HD), 0.5)


def draw_qkv_second(key, part):
    key = jax.random.fold_in(key, 32)
    return second_moment(key, (D, (QH + 2 * KVH) * HD), 0.5)


def draw_out_first(key, part):
    key = jax.random.fold_in(key, 33)
    return first_moment(key, (QH * HD, D), 1.0)


def draw_out_second(key, part):
    key = jax.random.fold_in(key, 34)
    return second_moment(key, (QH * HD, D), 1.0)


def draw_gate_up_first(key, part):
    key = jax.random.fold_in(key, 35)
    return first_moment(key, (2, D, FF), 0.5)


def draw_gate_up_second(key, part):
    key = jax.random.fold_in(key, 36)
    return second_moment(key, (2, D, FF), 0.5)


def draw_down_first(key, part):
    key = jax.random.fold_in(key, 37)
    return first_moment(key, (FF, D), 1.0)


def draw_down_second(key, part):
    key = jax.random.fold_in(key, 38)
    return second_moment(key, (FF, D), 1.0)


def draw_gains_first(key, part):
    key = jax.random.fold_in(key, 39)
    return first_moment(key, (D, 4), 2.0)


def draw_gains_second(key, part):
    key = jax.random.fold_in(key, 40)
    return second_moment(key, (D, 4), 2.0)


def with_spikes(drawn, own_key, source, target, shards_of, factor):
    owner, partner = [(jnp.arange(drawn.shape[dim]) // (drawn.shape[dim] // shards_of)).reshape([-1 if axis == dim else 1 for axis in range(drawn.ndim)]) for dim in (source, target)]
    chosen = jax.random.permutation(own_key, shards_of)[partner]
    strong = (owner == chosen) | (owner == (partner + shards_of // 2) % shards_of)
    return jnp.where(strong, factor * drawn, drawn)


def block_scale(rng, shape, cuts, least, largest):
    def one(dim, blocks):
        heights = jax.random.uniform(jax.random.fold_in(jax.random.fold_in(rng, 6), dim), (blocks,), jnp.float32, least / len(cuts), largest / len(cuts))
        return jnp.repeat(jnp.exp(heights), shape[dim] // blocks).reshape((-1,) + (1,) * (len(shape) - dim - 1))

    level = one(*cuts[0])
    for cut in cuts[1:]:
        level = level * one(*cut)
    return level


def scatter_about(rng, shape, width, most, cuts=(), kind=jnp.bfloat16):
    loudness = block_scale(rng, shape, cuts, -0.22, 0.18) if cuts else 1.0
    entries = jax.random.normal(rng, shape, jnp.float32) * width * loudness
    return jnp.minimum(jnp.maximum(entries, -most), most).astype(kind)


def gaussian_with(own_key, shape, scale, bound, cuts, heavy, held_as=jnp.bfloat16):
    values = scale * jax.random.normal(own_key, shape, jnp.float32)
    if cuts:
        values = values * block_scale(own_key, shape, cuts, -0.22, 0.18)
    return jnp.clip(with_spikes(values, jax.random.fold_in(own_key, 3), *heavy), -bound, bound).astype(held_as)


def setup_inputs(seed: int = 0) -> dict:
    key_list = jax.random.split(jax.random.key(seed), 19)
    return {
        "tokens": gaussian_with(key_list[0], (TOKENS, D), 1.0, 6.0, ((0, 32),), (0, 1, 32, 2.75)),
        "positions": draw_positions(jax.random.fold_in(key_list[18], 71), 0),
        "cotangent": scatter_about(key_list[2], (TOKENS, D), 1.0, 6.0, ((0, 32),)),
        "qkv_weight": scatter_about(key_list[3], (D, (QH + 2 * KVH) * HD), D ** -0.5, 0.125, ((0, 32),), jnp.float32),
        "qkv_first": draw_qkv_first(jax.random.fold_in(key_list[18], 71), 0),
        "qkv_second": draw_qkv_second(jax.random.fold_in(key_list[18], 71), 0),
        "out_weight": scatter_about(key_list[6], (QH * HD, D), (QH * HD) ** -0.5, 0.125, ((0, 32),), jnp.float32),
        "out_first": draw_out_first(jax.random.fold_in(key_list[18], 71), 0),
        "out_second": draw_out_second(jax.random.fold_in(key_list[18], 71), 0),
        "gate_up": scatter_about(key_list[9], (2, D, FF), D ** -0.5, 0.125, ((1, 8), (2, 4)), jnp.float32),
        "gate_up_first": draw_gate_up_first(jax.random.fold_in(key_list[18], 71), 0),
        "gate_up_second": draw_gate_up_second(jax.random.fold_in(key_list[18], 71), 0),
        "down_weight": scatter_about(key_list[12], (FF, D), FF ** -0.5, 0.0625, ((0, 4), (1, 8)), jnp.float32),
        "down_first": draw_down_first(jax.random.fold_in(key_list[18], 71), 0),
        "down_second": draw_down_second(jax.random.fold_in(key_list[18], 71), 0),
        "gains": jnp.clip(jax.random.uniform(key_list[15], (D, 4), jnp.float32, -0.6, 0.6) * block_scale(key_list[15], (D, 4), ((0, 32),), -0.4, 0.0), -0.6, 0.6),
        "gains_first": draw_gains_first(jax.random.fold_in(key_list[18], 71), 0),
        "gains_second": draw_gains_second(jax.random.fold_in(key_list[18], 71), 0),
    }


PRECISE = lax.Precision.HIGHEST
SOFT_CAP = 50.0
EPS_NORM = 1e-06
ROPE_BASE = 10000.0
BETA_ONE = 0.9
BETA_TWO = 0.95
EPS_ADAM = 1e-08
RATE_MATRIX = 0.05
RATE_DOWN = 0.025
RATE_GAIN = 0.5
WEIGHT_DECAY = 0.1

@jax.custom_vjp
def low(v):
    return lax.optimization_barrier(v.astype(jnp.bfloat16)).astype(jnp.float32)

@jax.custom_vjp
def low_back(v):
    return v

def low_keep(v):
    return (low(v), None)

def low_pass(kept, grad):
    return (grad,)

def back_keep(v):
    return (v, None)

def back_low(kept, grad):
    return (low(grad),)
low.defvjp(low_keep, low_pass)
low_back.defvjp(back_keep, back_low)

def matmul(left, right):
    return jnp.dot(left, right, precision=PRECISE, preferred_element_type=jnp.float32)

def rms_norm(values, gain_col):
    inv_scale = lax.rsqrt(lax.optimization_barrier(jnp.mean(values * values, axis=-1, keepdims=True)) + EPS_NORM)
    return values * inv_scale * (1.0 + gain_col)

def rope_tables(position, half_dim):
    freq_table = ROPE_BASE ** (-(jnp.arange(half_dim, dtype=jnp.float32) * 2.0 / (2 * half_dim)))
    angle_table = position.astype(jnp.float32)[:, None] * freq_table[None, :]
    return (jnp.cos(angle_table)[:, None, :], jnp.sin(angle_table)[:, None, :])

def rope_turn(values, cosine, sine_table):
    half_dim = values.shape[-1] // 2
    lead_half = values[..., :half_dim]
    tail_half = values[..., half_dim:]
    return jnp.concatenate([lead_half * cosine - tail_half * sine_table, tail_half * cosine + lead_half * sine_table], axis=-1)

def attend_block(query_block, query_pos, key_seq, value_seq, key_pos):
    scores = low_back(jnp.einsum('qkgd,rkd->kgqr', query_block, key_seq, precision=PRECISE))
    capped = SOFT_CAP * jnp.tanh(scores / SOFT_CAP)
    allowed = key_pos[None, None, None, :] <= query_pos[None, None, :, None]
    exp_scores = jnp.where(allowed, jnp.exp(capped), 0.0)
    exp_total = lax.optimization_barrier(jnp.sum(exp_scores, axis=-1))
    summed = low_back(jnp.einsum('kgqr,rkd->qkgd', low(exp_scores), value_seq, precision=PRECISE))
    return summed / jnp.transpose(exp_total, (2, 0, 1))[..., None]

def adam_step(weight, first_old, second_old, gradient, step_rate, decay_rate):
    first_new = BETA_ONE * first_old + (1.0 - BETA_ONE) * gradient
    second_new = BETA_TWO * second_old + (1.0 - BETA_TWO) * gradient * gradient
    first_hat = first_new / (1.0 - BETA_ONE ** STEP)
    second_hat = second_new / (1.0 - BETA_TWO ** STEP)
    weight_new = weight - step_rate * (first_hat / (jnp.sqrt(second_hat) + EPS_ADAM) + decay_rate * weight)
    return (first_new, second_new, weight_new)

def reference(tokens, positions, cotangent, qkv_weight, qkv_first, qkv_second, out_weight, out_first, out_second, gate_up, gate_up_first, gate_up_second, down_weight, down_first, down_second, gains, gains_first, gains_second):
    copies = max(1, N_HEAD // KVH)
    kv_copies = KVH * copies
    group_size = QH // kv_copies
    seq_count = TOKENS // SEQ
    query_rows = math.gcd(SEQ, 1024)
    cosine, sine_table = rope_tables(positions, HD // 2)
    query_scale = 1.0 / math.sqrt(HD)
    checked = jax.checkpoint(attend_block)

    def attend_sequence(seq_item):
        query_seq, key_seq, value_seq, pos_seq = seq_item
        query_blocks = query_seq.reshape(SEQ // query_rows, query_rows, kv_copies, group_size, HD)
        pos_blocks = pos_seq.reshape(SEQ // query_rows, query_rows)

        def one_block(block_item):
            return checked(block_item[0], block_item[1], key_seq, value_seq, pos_seq)
        return lax.map(one_block, (query_blocks, pos_blocks))

    def forward(inputs, qkv_full, out_full, gate_up_full, down_full, gain_full):
        gain_cols = low(gain_full)
        first_normed = low(rms_norm(inputs, gain_cols[:, 0]))
        projected = low_back(matmul(first_normed, low(qkv_full)))
        queries = rope_turn(projected[:, :QH * HD].reshape(TOKENS, QH, HD), cosine, sine_table) * query_scale
        key_rot = rope_turn(projected[:, QH * HD:(QH + KVH) * HD].reshape(TOKENS, KVH, HD), cosine, sine_table)
        values = projected[:, (QH + KVH) * HD:].reshape(TOKENS, KVH, HD)
        query_low = low_back(low(queries))
        key_copies = low_back(jnp.repeat(low(key_rot), copies, axis=1))
        value_copies = low_back(jnp.repeat(low(values), copies, axis=1))
        attended = lax.map(attend_sequence, (query_low.reshape(seq_count, SEQ, kv_copies, group_size, HD), key_copies.reshape(seq_count, SEQ, kv_copies, HD), value_copies.reshape(seq_count, SEQ, kv_copies, HD), positions.reshape(seq_count, SEQ)))
        attended = low_back(low(attended.reshape(TOKENS, QH * HD)))
        attn_out = low_back(matmul(attended, low(out_full)))
        middle = inputs + rms_norm(attn_out, gain_cols[:, 1])
        second_normed = low(rms_norm(middle, gain_cols[:, 2]))
        gate_act = low_back(matmul(second_normed, low(gate_up_full[0])))
        up_act = low_back(matmul(second_normed, low(gate_up_full[1])))
        hidden = low(jax.nn.gelu(gate_act, approximate=True) * up_act)
        ffn_out = low_back(matmul(hidden, low(down_full)))
        return middle + rms_norm(ffn_out, gain_cols[:, 3])
    output_rows, pullback = jax.vjp(forward, tokens.astype(jnp.float32), qkv_weight, out_weight, gate_up, down_weight, gains)
    gradients = pullback(cotangent.astype(jnp.float32))
    grad_inputs, qkv_grad, out_grad, gate_up_grad, down_grad, gains_grad = gradients
    qkv_first_new, qkv_second_new, qkv_new = adam_step(qkv_weight, qkv_first, qkv_second, qkv_grad, RATE_MATRIX, WEIGHT_DECAY)
    out_first_new, out_second_new, out_new = adam_step(out_weight, out_first, out_second, out_grad, RATE_MATRIX, WEIGHT_DECAY)
    gate_up_first_new, gate_up_second_new, gate_up_new = adam_step(gate_up, gate_up_first, gate_up_second, gate_up_grad, RATE_MATRIX, WEIGHT_DECAY)
    down_first_new, down_second_new, down_new = adam_step(down_weight, down_first, down_second, down_grad, RATE_DOWN, WEIGHT_DECAY)
    gains_first_new, gains_second_new, gains_new = adam_step(gains, gains_first, gains_second, gains_grad, RATE_GAIN, 0.0)
    return (output_rows.astype(jnp.bfloat16), grad_inputs.astype(jnp.bfloat16), qkv_grad, qkv_first_new, qkv_second_new, qkv_new, out_grad, out_first_new, out_second_new, out_new, gate_up_grad, gate_up_first_new, gate_up_second_new, gate_up_new, down_grad, down_first_new, down_second_new, down_new, gains_grad, gains_first_new, gains_second_new, gains_new)
```

```python
import math

import jax
import jax.numpy as jnp
from jax import lax
from jax.sharding import PartitionSpec as P

QH = 8
KVH = 4
HD = 256
STEP = 10


SOFT_CAP = 50.0
EPS_NORM = 1e-06
ROPE_BASE = 10000.0
BETA_ONE = 0.9
BETA_TWO = 0.95
EPS_ADAM = 1e-08
RATE_MATRIX = 0.05
RATE_DOWN = 0.025
RATE_GAIN = 0.5
WEIGHT_DECAY = 0.1

BF16 = jnp.bfloat16
F32 = jnp.float32


def send_by(values, axis, step):
    size = lax.axis_size(axis)
    return lax.ppermute(values, axis, [(i, (i + step) % size) for i in range(size)])


def swap_bit(values, axis, bit):
    size = lax.axis_size(axis)
    return lax.ppermute(values, axis, [(i, i ^ bit) for i in range(size)])


def head_bits():
    bits = []
    bit = lax.axis_size("head") // 2
    while bit:
        bits.append(bit)
        bit //= 2
    return bits


def head_order():
    order = [0]
    for bit in head_bits():
        order = order + [one ^ bit for one in order]
    return order


def head_gather(rows):
    for bit in head_bits():
        rows = jnp.concatenate([rows, swap_bit(rows, "head", bit)], axis=0)
    return rows


def head_reduce(part):
    for bit in reversed(head_bits()):
        half = part.shape[0] // 2
        came = swap_bit(part[half:].astype(BF16), "head", bit)
        part = part[:half].astype(F32) + came.astype(F32)
    return part


def head_exchange(pieces):
    size = lax.axis_size("head")
    own = lax.axis_index("head")
    result = pieces
    for other in range(1, size):
        came = swap_bit(lax.dynamic_index_in_dim(pieces, own ^ other, 0, keepdims=True), "head", other)
        result = lax.dynamic_update_slice_in_dim(result, came, own ^ other, 0)
    return result


def gather_pieces(piece_for):
    size_x, size_z = lax.axis_size("fsdp"), lax.axis_size("ctx")
    x, z = lax.axis_index("fsdp"), lax.axis_index("ctx")
    own = piece_for(0)
    result = jnp.zeros((size_x, size_z) + own.shape, own.dtype)
    for k in range(size_z):
        came = own if k == 0 else send_by(piece_for(k), "ctx", k)
        place = lax.rem(z - k + size_z, size_z)
        result = lax.dynamic_update_slice(result, came[None, None], (x, place) + (0,) * own.ndim)
        for step in range(1, size_x):
            other = send_by(came, "fsdp", step)
            place_x = lax.rem(x - step + size_x, size_x)
            result = lax.dynamic_update_slice(
                result, other[None, None], (place_x, place) + (0,) * own.ndim
            )
    return result


def scatter_pieces(pieces):
    size_x, size_z = lax.axis_size("fsdp"), lax.axis_size("ctx")
    x, z = lax.axis_index("fsdp"), lax.axis_index("ctx")
    rest = pieces.shape[2:]

    def pick(at_x, at_z):
        return lax.dynamic_slice(
            pieces, (at_x, at_z) + (0,) * len(rest), (1, 1) + rest
        ).reshape(rest)

    came_by = [None] * size_z
    for k in sorted(range(size_z), key=lambda k: -min(k, size_z - k)):
        at_z = lax.rem(z + k, size_z)
        total = pick(x, at_z).astype(F32)
        for step in range(1, size_x):
            at_x = lax.rem(x + step, size_x)
            total = total + send_by(pick(at_x, at_z).astype(BF16), "fsdp", step).astype(F32)
        came_by[k] = total if k == 0 else send_by(total.astype(BF16), "ctx", k).astype(F32)
    return came_by


def gather_gains(gains):
    rows = gains.astype(BF16).T
    for axis in ("head", "ctx", "fsdp"):
        size, bit = lax.axis_size(axis), 1
        own = lax.axis_index(axis)
        while bit < size:
            other = swap_bit(rows, axis, bit)
            rows = jnp.where(
                (own & bit) == 0,
                jnp.concatenate([rows, other], axis=1),
                jnp.concatenate([other, rows], axis=1),
            )
            bit *= 2
    return rows.astype(F32)


def scatter_gains(rows):
    for axis in ("fsdp", "ctx", "head"):
        own = lax.axis_index(axis)
        bit = lax.axis_size(axis) // 2
        while bit:
            half = rows.shape[1] // 2
            low_part, high_part = rows[:, :half], rows[:, half:]
            is_low = (own & bit) == 0
            keep = jnp.where(is_low, low_part, high_part)
            rows = keep + swap_bit(jnp.where(is_low, high_part, low_part), axis, bit)
            bit //= 2
    return rows.T


def matmul(left, right):
    return jnp.dot(left, right, preferred_element_type=F32)


def matmul_nt(left, right):
    return lax.dot_general(left, right, (((1,), (1,)), ((), ())), preferred_element_type=F32)


def matmul_tn(left, right):
    return lax.dot_general(left, right, (((0,), (0,)), ((), ())), preferred_element_type=F32)


def rms_norm(values, gain_row):
    inv_scale = lax.rsqrt(jnp.mean(values * values, axis=-1, keepdims=True) + EPS_NORM)
    return values * inv_scale * (1.0 + gain_row)


def norm_back(values, gain_row, upstream):
    inv_scale = lax.rsqrt(jnp.mean(values * values, axis=-1, keepdims=True) + EPS_NORM)
    unit_rows = values * inv_scale
    scaled = upstream * (1.0 + gain_row)
    result = inv_scale * (scaled - unit_rows * jnp.mean(scaled * unit_rows, axis=-1, keepdims=True))
    return (result, jnp.sum(upstream * unit_rows, axis=0))


def rope_tables(position, half_dim):
    freq_table = ROPE_BASE ** (-(jnp.arange(half_dim, dtype=F32) * 2.0 / (2 * half_dim)))
    angle_table = position.astype(F32)[:, None] * freq_table[None, :]
    return (jnp.cos(angle_table), jnp.sin(angle_table))


def rope_turn(values, cosine, sine_table):
    half_dim = values.shape[-1] // 2
    lead_half = values[..., :half_dim]
    tail_half = values[..., half_dim:]
    return jnp.concatenate(
        [lead_half * cosine - tail_half * sine_table, tail_half * cosine + lead_half * sine_table],
        axis=-1,
    )


def rope_back(grad_rows, cosine, sine_table):
    return rope_turn(grad_rows, cosine, -sine_table)


def gated_unit(gate_in, up_in):
    return jax.nn.gelu(gate_in, approximate=True) * up_in


def adam_step(weight, first_old, second_old, gradient, step_rate, decay_rate):
    first_new = BETA_ONE * first_old + (1.0 - BETA_ONE) * gradient
    second_new = BETA_TWO * second_old + (1.0 - BETA_TWO) * gradient * gradient
    first_hat = first_new / (1.0 - BETA_ONE**STEP)
    second_hat = second_new / (1.0 - BETA_TWO**STEP)
    weight_new = weight - step_rate * (
        first_hat / (jnp.sqrt(second_hat) + EPS_ADAM) + decay_rate * weight
    )
    return (first_new, second_new, weight_new)


def block_weights(queries, keys, query_pos, key_pos):
    scores = jnp.einsum("kqd,krd->kqr", queries, keys, preferred_element_type=F32)
    unit = jnp.tanh(scores / SOFT_CAP)
    allowed = key_pos[None, None, :] <= query_pos[None, :, None]
    return (unit, jnp.where(allowed, jnp.exp(SOFT_CAP * unit), 0.0))


def block_forward(queries, keys, values, query_pos, key_pos):
    unused, weights = block_weights(queries, keys, query_pos, key_pos)
    return (
        jnp.sum(weights, axis=-1, keepdims=True),
        jnp.einsum("kqr,krd->kqd", weights.astype(BF16), values, preferred_element_type=F32),
    )


def block_backward(queries, keys, values, query_pos, key_pos, grad_summed, delta):
    unit, weights = block_weights(queries, keys, query_pos, key_pos)
    grad_weights = jnp.einsum("kqd,krd->kqr", grad_summed, values, preferred_element_type=F32)
    grad_scores = (weights * (grad_weights - delta) * (1.0 - unit * unit)).astype(BF16)
    return (
        jnp.einsum("kqr,krd->kqd", grad_scores, keys, preferred_element_type=F32),
        jnp.einsum("kqr,kqd->krd", grad_scores, queries, preferred_element_type=F32),
        jnp.einsum("kqr,kqd->krd", weights.astype(BF16), grad_summed, preferred_element_type=F32),
    )


def shards(
    tokens,
    positions,
    cotangent,
    qkv_weight,
    qkv_first,
    qkv_second,
    out_weight,
    out_first,
    out_second,
    gate_up,
    gate_up_first,
    gate_up_second,
    down_weight,
    down_first,
    down_second,
    gains,
    gains_first,
    gains_second,
):
    size_x, size_z, size_h = lax.axis_size("fsdp"), lax.axis_size("ctx"), lax.axis_size("head")
    z, own_h = lax.axis_index("ctx"), lax.axis_index("head")
    tok_rows, width = tokens.shape
    block_rows = tok_rows * size_h
    order = head_order()
    copies = max(1, size_h // KVH)
    kv_local = KVH * copies // size_h
    query_local = QH // size_h
    group = query_local // kv_local
    query_scale = 1.0 / math.sqrt(HD)
    query_cols, kv_cols = query_local * HD, kv_local * HD

    def positions_of(block):
        rows = lax.dynamic_slice_in_dim(positions, block * block_rows, block_rows)
        return jnp.concatenate(
            [lax.dynamic_slice_in_dim(rows, (own_h ^ one) * tok_rows, tok_rows) for one in order]
        )

    qkv_rows = qkv_weight.shape[0]
    qkv_low = qkv_weight.astype(BF16)

    def head_columns(part, heads, repeat):
        part = jnp.repeat(part.reshape(qkv_rows, heads, HD), repeat, axis=1)
        return part.reshape(qkv_rows, size_h, heads * repeat // size_h * HD)

    by_head = jnp.concatenate(
        [
            head_columns(qkv_low[:, : QH * HD], QH, 1),
            head_columns(qkv_low[:, QH * HD : (QH + KVH) * HD], KVH, copies),
            head_columns(qkv_low[:, (QH + KVH) * HD :], KVH, copies),
        ],
        axis=2,
    )
    local_cols = by_head.shape[2]
    qkv_piece = head_exchange(jnp.transpose(by_head, (1, 0, 2))).reshape(
        size_h * qkv_rows, local_cols
    )
    qkv_full = gather_pieces(lambda k: qkv_piece).reshape(width, local_cols)

    out_rows = out_weight.shape[0]
    strip = width // size_h
    out_low = jnp.transpose(out_weight.astype(BF16).reshape(out_rows, size_h, strip), (1, 0, 2))
    out_piece = head_exchange(out_low).reshape(size_h * out_rows, strip)
    out_strip = gather_pieces(lambda k: out_piece).reshape(size_h, query_cols, strip)
    out_full = jnp.transpose(head_exchange(out_strip), (1, 0, 2)).reshape(query_cols, width)

    gain_rows = gather_gains(gains)

    ff_rows = gate_up.shape[1]
    ff_cols = gate_up.shape[2] // size_z
    gate_up_low = jnp.transpose(
        gate_up.astype(BF16).reshape(2, ff_rows, size_z, ff_cols), (2, 1, 0, 3)
    ).reshape(size_z, ff_rows, 2 * ff_cols)
    down_low = jnp.transpose(
        down_weight.astype(BF16).reshape(size_z, ff_cols, ff_rows), (0, 2, 1)
    )
    gate_up_full = gather_pieces(
        lambda k: lax.dynamic_index_in_dim(gate_up_low, lax.rem(z + k, size_z), 0, keepdims=False)
    ).reshape(width, 2 * ff_cols)
    down_full = gather_pieces(
        lambda k: lax.dynamic_index_in_dim(down_low, lax.rem(z + k, size_z), 0, keepdims=False)
    ).reshape(width, ff_cols)

    block_tokens = head_gather(tokens).astype(F32)
    inputs = tokens.astype(F32)
    first_normed = rms_norm(block_tokens, gain_rows[0]).astype(BF16)
    projected = matmul(first_normed, qkv_full)
    block_pos = positions_of(z)
    cosine, sine_table = rope_tables(block_pos, HD // 2)

    def heads_of(values, count):
        return jnp.transpose(values.reshape(block_rows, count, HD), (1, 0, 2))

    queries = heads_of(projected[:, :query_cols], query_local)
    queries = (rope_turn(queries, cosine, sine_table) * query_scale).astype(BF16)
    queries = queries.reshape(kv_local, group * block_rows, HD)
    own_keys = heads_of(projected[:, query_cols : query_cols + kv_cols], kv_local)
    own_keys = rope_turn(own_keys, cosine, sine_table).astype(BF16)
    own_values = heads_of(projected[:, query_cols + kv_cols :], kv_local).astype(BF16)
    query_pos = jnp.tile(block_pos, group)
    own_kv = jnp.stack([own_keys, own_values])
    kv_slots = [own_kv] + [send_by(own_kv, "ctx", k) for k in range(1, size_z)]
    pos_slots = [positions_of(lax.rem(z - k + size_z, size_z)) for k in range(size_z)]
    exp_total = 0.0
    summed = 0.0
    for kv_slot, key_pos in zip(kv_slots, pos_slots):
        total_part, summed_part = block_forward(
            queries, kv_slot[0], kv_slot[1], query_pos, key_pos
        )
        exp_total = exp_total + total_part
        summed = summed + summed_part
    attended = summed / exp_total

    def rows_of(heads):
        heads = heads.reshape(-1, block_rows, HD)
        return jnp.transpose(heads, (1, 0, 2)).reshape(block_rows, -1)

    attended_low = rows_of(attended.astype(BF16))
    attn_out = head_reduce(matmul(attended_low, out_full).astype(BF16))
    middle = inputs + rms_norm(attn_out, gain_rows[1])
    second_normed = rms_norm(middle, gain_rows[2]).astype(BF16)

    def all_slots(rows):
        return [head_gather(rows)] + [
            head_gather(send_by(rows, "ctx", k)) for k in range(1, size_z)
        ]

    def sum_slots(parts):
        total = head_reduce(parts[0])
        for k in range(1, size_z):
            back = send_by(head_reduce(parts[k]).astype(BF16), "ctx", size_z - k)
            total = total + back.astype(F32)
        return total

    normed_slots = all_slots(second_normed)
    act_slots = [matmul(rows, gate_up_full) for rows in normed_slots]
    hidden_slots = [
        gated_unit(act[:, :ff_cols], act[:, ff_cols:]).astype(BF16) for act in act_slots
    ]
    ffn_out = sum_slots([matmul_nt(hidden, down_full).astype(BF16) for hidden in hidden_slots])
    mixed_out = (middle + rms_norm(ffn_out, gain_rows[3])).astype(BF16)

    upstream = cotangent.astype(F32)
    grad_ffn, gain_grad_ffn = norm_back(ffn_out, gain_rows[3], upstream)
    grad_slots = all_slots(grad_ffn.astype(BF16))
    grad_act_slots = []
    for rows, act in zip(grad_slots, act_slots):
        grad_hidden = matmul(rows, down_full)
        unit_out, unit_back = jax.vjp(gated_unit, act[:, :ff_cols], act[:, ff_cols:])
        grad_act_slots.append(jnp.concatenate(unit_back(grad_hidden), axis=1).astype(BF16))
    grad_second = sum_slots([matmul_nt(rows, gate_up_full).astype(BF16) for rows in grad_act_slots])
    down_term = matmul_tn(jnp.concatenate(grad_slots), jnp.concatenate(hidden_slots))
    gate_up_term = matmul_tn(jnp.concatenate(normed_slots), jnp.concatenate(grad_act_slots))
    down_came = scatter_pieces(down_term.reshape(size_x, size_z, ff_rows, ff_cols))
    gate_up_came = scatter_pieces(gate_up_term.reshape(size_x, size_z, ff_rows, 2 * ff_cols))

    def in_order(came):
        result = jnp.zeros((size_z,) + came[0].shape, F32)
        for k, part in enumerate(came):
            result = lax.dynamic_update_slice_in_dim(
                result, part[None], lax.rem(z - k + size_z, size_z), 0
            )
        return result

    down_grad = jnp.transpose(in_order(down_came), (0, 2, 1)).reshape(down_weight.shape)
    gate_up_grad = jnp.transpose(
        in_order(gate_up_came).reshape(size_z, ff_rows, 2, ff_cols), (2, 1, 0, 3)
    ).reshape(gate_up.shape)

    grad_middle_part, gain_grad_middle = norm_back(middle, gain_rows[2], grad_second)
    grad_middle = upstream + grad_middle_part
    grad_attn, gain_grad_attn = norm_back(attn_out, gain_rows[1], grad_middle)
    block_grad_attn = head_gather(grad_attn.astype(BF16))
    out_term = matmul_tn(attended_low, block_grad_attn).astype(BF16)
    out_term = head_exchange(
        jnp.transpose(out_term.reshape(query_cols, size_h, strip), (1, 0, 2))
    )
    out_came = sum(scatter_pieces(out_term.reshape(size_x, size_z, size_h * out_rows, strip)))
    out_grad = head_exchange(out_came.reshape(size_h, out_rows, strip).astype(BF16)).astype(F32)
    out_grad = jnp.transpose(out_grad, (1, 0, 2)).reshape(out_weight.shape)

    grad_attended = matmul_nt(block_grad_attn, out_full).astype(BF16)
    grad_attended = heads_of(grad_attended, query_local).astype(F32)
    grad_attended = grad_attended.reshape(kv_local, group * block_rows, HD)
    row_delta = jnp.sum(grad_attended * attended, axis=-1, keepdims=True)
    delta = row_delta / exp_total
    grad_summed = (grad_attended / exp_total).astype(BF16)
    grad_query = 0.0
    grad_kv = 0.0
    for k in sorted(range(size_z), key=lambda k: -min(k, size_z - k)):
        query_part, key_part, value_part = block_backward(
            queries, kv_slots[k][0], kv_slots[k][1], query_pos, pos_slots[k], grad_summed, delta
        )
        grad_query = grad_query + query_part
        kv_part = jnp.stack([key_part, value_part])
        if k:
            kv_part = send_by(kv_part.astype(BF16), "ctx", size_z - k).astype(F32)
        grad_kv = grad_kv + kv_part
    grad_query = grad_query.astype(BF16).astype(F32).reshape(query_local, block_rows, HD)
    grad_kv = grad_kv.astype(BF16).astype(F32)
    grad_proj = jnp.concatenate(
        [
            rows_of(rope_back(grad_query, cosine, sine_table) * query_scale),
            rows_of(rope_back(grad_kv[0], cosine, sine_table)),
            rows_of(grad_kv[1]),
        ],
        axis=1,
    ).astype(BF16)
    grad_first = head_reduce(matmul_nt(grad_proj, qkv_full).astype(BF16))
    grad_input_part, gain_grad_input = norm_back(inputs, gain_rows[0], grad_first)
    tokens_grad = (grad_middle + grad_input_part).astype(BF16)

    qkv_term = matmul_tn(first_normed, grad_proj)
    qkv_came = sum(scatter_pieces(qkv_term.reshape(size_x, size_z, size_h * qkv_rows, local_cols)))
    qkv_grad = head_exchange(qkv_came.reshape(size_h, qkv_rows, local_cols).astype(BF16))
    qkv_grad = jnp.transpose(qkv_grad.astype(F32), (1, 0, 2))

    def whole_columns(part, heads, repeat):
        part = part.reshape(qkv_rows, heads, repeat, HD)
        return jnp.sum(part, axis=2).reshape(qkv_rows, heads * HD)

    qkv_grad = jnp.concatenate(
        [
            whole_columns(qkv_grad[:, :, :query_cols], QH, 1),
            whole_columns(qkv_grad[:, :, query_cols : query_cols + kv_cols], KVH, copies),
            whole_columns(qkv_grad[:, :, query_cols + kv_cols :], KVH, copies),
        ],
        axis=1,
    )
    gains_grad = scatter_gains(
        jnp.stack([gain_grad_input, gain_grad_attn, gain_grad_middle, gain_grad_ffn])
    )

    qkv_first_new, qkv_second_new, qkv_new = adam_step(
        qkv_weight, qkv_first, qkv_second, qkv_grad, RATE_MATRIX, WEIGHT_DECAY
    )
    out_first_new, out_second_new, out_new = adam_step(
        out_weight, out_first, out_second, out_grad, RATE_MATRIX, WEIGHT_DECAY
    )
    gate_up_first_new, gate_up_second_new, gate_up_new = adam_step(
        gate_up, gate_up_first, gate_up_second, gate_up_grad, RATE_MATRIX, WEIGHT_DECAY
    )
    down_first_new, down_second_new, down_new = adam_step(
        down_weight, down_first, down_second, down_grad, RATE_DOWN, WEIGHT_DECAY
    )
    gains_first_new, gains_second_new, gains_new = adam_step(
        gains, gains_first, gains_second, gains_grad, RATE_GAIN, 0.0
    )
    return (
        mixed_out,
        tokens_grad,
        qkv_grad,
        qkv_first_new,
        qkv_second_new,
        qkv_new,
        out_grad,
        out_first_new,
        out_second_new,
        out_new,
        gate_up_grad,
        gate_up_first_new,
        gate_up_second_new,
        gate_up_new,
        down_grad,
        down_first_new,
        down_second_new,
        down_new,
        gains_grad,
        gains_first_new,
        gains_second_new,
        gains_new,
    )


TOKEN_SPEC = P(("fsdp", "ctx", "head"), None)
GATE_UP_SPEC = P(None, ("fsdp", "ctx"), "head")
DOWN_SPEC = P("head", ("fsdp", "ctx"))


def solution(mesh):
    in_specs = (
        (TOKEN_SPEC, P("fsdp"))
        + (TOKEN_SPEC,) * 7
        + (GATE_UP_SPEC,) * 3
        + (DOWN_SPEC,) * 3
        + (TOKEN_SPEC,) * 3
    )
    out_specs = (
        (TOKEN_SPEC,) * 10 + (GATE_UP_SPEC,) * 4 + (DOWN_SPEC,) * 4 + (TOKEN_SPEC,) * 4
    )
    return jax.shard_map(shards, mesh=mesh, in_specs=in_specs, out_specs=out_specs, check_vma=False)
```

```python
import functools
import math

import jax
import jax.numpy as jnp
from jax import lax
from jax.experimental import pallas as pl
from jax.experimental.pallas import tpu as pltpu
from jax.sharding import PartitionSpec as P

QH = 8
KVH = 4
HD = 256
STEP = 10


SOFT_CAP = 50.0
EPS_NORM = 1e-06
ROPE_BASE = 10000.0
BETA_ONE = 0.9
BETA_TWO = 0.95
EPS_ADAM = 1e-08
RATE_MATRIX = 0.05
RATE_DOWN = 0.025
RATE_GAIN = 0.5
WEIGHT_DECAY = 0.1

BF16 = jnp.bfloat16
F32 = jnp.float32


def after(values, *others):
    return lax.optimization_barrier((values,) + others)[0]


class Line:
    def __init__(self, depth):
        self.depth = depth
        self.came = []

    def send(self, sendings):
        values = tuple(one for one, _, _ in sendings)
        if len(self.came) >= self.depth:
            values = after(values, *self.came[-self.depth])
        results = [
            lax.ppermute(one, axes, pairs) for one, (_, axes, pairs) in zip(values, sendings)
        ]
        self.came.append(tuple(results))
        return results


class Lines:
    def __init__(self):
        self.fsdp, self.ctx, self.head = Line(DEPTH), Line(DEPTH), Line(DEPTH)


DEPTH = 2


def ring_pairs(size, step):
    return [(i, (i + step) % size) for i in range(size)]


def swap_bit(lines, values, bit):
    size = lax.axis_size("head")
    pairs = [(i, i ^ bit) for i in range(size)]
    if bit == 1 and size > 2:
        return lax.ppermute(values, "head", pairs)
    return lines.head.send([(values, "head", pairs)])[0]


def send_ctx(lines, values, step):
    return lines.ctx.send([(values, "ctx", ring_pairs(lax.axis_size("ctx"), step))])[0]


def swap_fsdp(lines, values, valid=lambda z: True):
    size_x, size_z = lax.axis_size("fsdp"), lax.axis_size("ctx")
    return [
        lines.fsdp.send(
            [
                (
                    values,
                    ("fsdp", "ctx"),
                    [
                        (x * size_z + z, (x + step) % size_x * size_z + z)
                        for x in range(size_x)
                        for z in range(size_z)
                        if valid(z)
                    ],
                )
            ]
        )[0]
        for step in range(1, size_x)
    ]


def swap_top(lines, values, valid=lambda z: True):
    size_z, size_h = lax.axis_size("ctx"), lax.axis_size("head")
    pairs = [
        (z * size_h + h, z * size_h + (h ^ (size_h // 2)))
        for z in range(size_z)
        for h in range(size_h)
        if valid(z)
    ]
    return lines.head.send([(values, ("ctx", "head"), pairs)])


def head_bits():
    bits = []
    bit = lax.axis_size("head") // 2
    while bit:
        bits.append(bit)
        bit //= 2
    return bits


def head_order():
    order = [0]
    for bit in head_bits():
        order = order + [one ^ bit for one in order]
    return order


def head_gather(lines, rows, bits=None):
    for bit in head_bits() if bits is None else bits:
        rows = jnp.concatenate([rows, swap_bit(lines, rows, bit)], axis=0)
    return rows


def head_reduce(lines, part):
    for bit in reversed(head_bits()):
        half = part.shape[0] // 2
        came = swap_bit(lines, part[half:].astype(BF16), bit)
        part = part[:half].astype(F32) + came.astype(F32)
    return part


def head_exchange(lines, pieces):
    return [pieces[0]] + [swap_bit(lines, pieces[i], i) for i in range(1, len(pieces))]


AHEAD, BACK = [(0, 1), (1, 2), (2, 3)], [(1, 0), (2, 1), (3, 2)]
TWO, ENDS = [(0, 2), (1, 3), (2, 0), (3, 1)], [(2, 3), (1, 0)]
FAR = [(0, 1), (3, 2)]


def spread_ctx(lines, own, swaps):
    size = lax.axis_size("ctx")
    always = lambda z: z >= 0
    parts = [([own] + swaps(lines, own), lambda z: z, always)]
    if size != 4:
        for k in range(1, size):
            one = send_ctx(lines, own, k)
            source = lambda z, k=k: (z - k + size) % size
            parts.append(([one] + swaps(lines, one), source, always))
        return parts
    not_first, not_last, at_end = lambda z: z >= 1, lambda z: z <= 2, lambda z: z % 3 == 0
    ahead, back = lines.ctx.send([(own, "ctx", AHEAD), (own, "ctx", BACK)])
    two = lines.ctx.send([(after(own, ahead, back), "ctx", TWO)])[0]
    parts.append(([ahead] + swaps(lines, ahead, not_first), lambda z: z - 1, not_first))
    parts.append(([back] + swaps(lines, back, not_last), lambda z: z + 1, not_last))
    two = after(two, *parts[1][0][1:])
    ends = lines.ctx.send([(two, "ctx", ENDS)])[0]
    parts.append(([two] + swaps(lines, two), lambda z: z ^ 2, always))
    parts.append(([ends] + swaps(lines, ends, at_end), lambda z: 3 - z, at_end))
    return parts


def put_pieces(parts):
    size_x, size_z = lax.axis_size("fsdp"), lax.axis_size("ctx")
    x, z = lax.axis_index("fsdp"), lax.axis_index("ctx")
    arrays, places = [], []
    for by_step, source, valid in parts:
        for step, one in enumerate(by_step):
            at = lax.rem(x - step + size_x, size_x) * size_z + source(z)
            arrays.append(one)
            places.append(jnp.where(valid(z), at, -1))
    return place(arrays, places, size_x * size_z)


def ctx_slots(lines, values, swaps=lambda lines, values, valid=None: [], join=lambda arrays: arrays[0]):
    size = lax.axis_size("ctx")
    arrays = [join(by_step) for by_step, _, _ in spread_ctx(lines, values, swaps)]
    if size != 4:
        return [arrays[0]] + [arrays[size - k] for k in range(1, size)]
    z = lax.axis_index("ctx")
    own, ahead, back, two, ends = arrays
    return [own, jnp.where(z == 3, ends, back), two, jnp.where(z == 0, ends, ahead)]


def sum_ctx_slots(lines, part_of):
    size = lax.axis_size("ctx")
    z = lax.axis_index("ctx")
    if size != 4:
        total = 0.0
        for k in ctx_order():
            part = part_of(k)
            total = total + (send_ctx(lines, part.astype(BF16), k).astype(F32) if k else part)
        return total
    part_one = part_of(1).astype(BF16)
    part_three = part_of(3).astype(BF16)
    far = lines.ctx.send([(jnp.where(z == 0, part_three, part_one), "ctx", FAR)])[0]
    ahead, back = lines.ctx.send([(part_one, "ctx", AHEAD), (part_three, "ctx", BACK)])
    part_two = part_of(2).astype(F32) + far.astype(F32)
    two = lines.ctx.send([(part_two.astype(BF16), "ctx", TWO)])[0]
    return part_of(0).astype(F32) + ahead.astype(F32) + back.astype(F32) + two.astype(F32)


def far_first(size):
    return sorted(range(size), key=lambda k: -min(k, size - k))


def ctx_order():
    size = lax.axis_size("ctx")
    return [1, 3, 2, 0] if size == 4 else far_first(size)


def sum_over_fsdp(lines, pieces, order):
    size_x, size_z = lax.axis_size("fsdp"), lax.axis_size("ctx")
    x, z = lax.axis_index("fsdp"), lax.axis_index("ctx")
    chosen = [(k, step) for k in order for step in range(size_x)]
    picked = pick_pieces(
        pieces,
        [lax.rem(x + step, size_x) * size_z + lax.rem(z + k, size_z) for k, step in chosen],
    )
    picked = dict(zip(chosen, picked))
    sums = {}
    for k in order:
        total = picked[k, 0].astype(F32)
        for step in range(1, size_x):
            pairs = ring_pairs(size_x, step)
            total = total + lines.fsdp.send([(picked[k, step], "fsdp", pairs)])[0].astype(F32)
        sums[k] = total
    return sums


def exchange_all(pieces):
    return lax.all_to_all(
        pieces, ("fsdp", "ctx", "head"), split_axis=0, concat_axis=0, tiled=True
    )


def device_count():
    return lax.axis_size("fsdp") * lax.axis_size("ctx") * lax.axis_size("head")


def gather_gains(gains):
    rows = exchange_all(jnp.broadcast_to(gains.astype(BF16).T[None], (device_count(),) + gains.shape[::-1]))
    return jnp.transpose(rows, (1, 0, 2)).reshape(gains.shape[1], -1).astype(F32)


def scatter_gains(rows):
    pieces = jnp.transpose(rows.reshape(rows.shape[0], device_count(), -1), (1, 0, 2))
    return jnp.sum(exchange_all(pieces), axis=0).T


ANYWHERE = pl.BlockSpec(memory_space=pl.ANY)
SCALARS = pl.BlockSpec(memory_space=pltpu.SMEM)
IN_VMEM = pl.BlockSpec(memory_space=pltpu.VMEM)
VMEM_LIMIT = 48 * 1024 * 1024


def scalars(*values):
    return jnp.stack([jnp.asarray(one, jnp.int32) for one in values])


def cost(byte_count, flops=0):
    return pl.CostEstimate(flops=flops, bytes_accessed=byte_count, transcendentals=0)


def params():
    return pltpu.CompilerParams(vmem_limit_bytes=VMEM_LIMIT)


def place(pieces, places, total=None):
    count = len(pieces)
    shape = (total or count,) + pieces[0].shape

    def kernel(places_ref, *refs):
        out_ref, sems = refs[count], refs[count + 1]

        def each(act):
            for i in range(count):
                copy = pltpu.make_async_copy(
                    refs[i], out_ref.at[jnp.maximum(places_ref[i], 0)], sems.at[i]
                )
                pl.when(places_ref[i] >= 0)(functools.partial(act, copy))

        each(lambda copy: copy.start())
        each(lambda copy: copy.wait())

    return pl.pallas_call(
        kernel,
        out_shape=jax.ShapeDtypeStruct(shape, pieces[0].dtype),
        in_specs=[SCALARS] + [ANYWHERE] * count,
        out_specs=IN_VMEM,
        scratch_shapes=[pltpu.SemaphoreType.DMA((count,))],
        compiler_params=params(),
        cost_estimate=cost(2 * math.prod(shape) * pieces[0].dtype.itemsize),
        name="place",
    )(scalars(*places), *pieces)


def pick_pieces(stacked, places):
    count = len(places)
    shape = stacked.shape[1:]

    def kernel(places_ref, in_ref, *refs):
        sems = refs[count]
        copies = [
            pltpu.make_async_copy(in_ref.at[places_ref[i]], refs[i], sems.at[i])
            for i in range(count)
        ]
        for copy in copies:
            copy.start()
        for copy in copies:
            copy.wait()

    return pl.pallas_call(
        kernel,
        out_shape=[jax.ShapeDtypeStruct(shape, stacked.dtype)] * count,
        in_specs=[SCALARS, IN_VMEM],
        out_specs=[ANYWHERE] * count,
        scratch_shapes=[pltpu.SemaphoreType.DMA((count,))],
        compiler_params=params(),
        cost_estimate=cost(2 * count * math.prod(shape) * stacked.dtype.itemsize),
        name="pick_pieces",
    )(scalars(*places), stacked)


def kv_start(head):
    return lax.div(head * KVH, lax.axis_size("head")) * HD


def split_heads(weight, own):
    rows = weight.shape[0]
    size = lax.axis_size("head")
    query_cols, kv_cols = QH * HD // size, max(1, KVH // size) * HD
    local_cols = query_cols + 2 * kv_cols

    def kernel(own_ref, weight_ref, *outs):
        for other in range(size):
            head = own_ref[0] ^ other
            starts = (head * query_cols, QH * HD + kv_start(head), (QH + KVH) * HD + kv_start(head))
            at = 0
            for start, count in zip(starts, (query_cols, kv_cols, kv_cols)):
                columns = pl.ds(pl.multiple_of(start, HD), count)
                outs[other][:, at : at + count] = weight_ref[:, columns].astype(BF16)
                at += count

    return pl.pallas_call(
        kernel,
        out_shape=[jax.ShapeDtypeStruct((rows, local_cols), BF16)] * size,
        in_specs=[SCALARS, IN_VMEM],
        out_specs=[IN_VMEM] * size,
        compiler_params=params(),
        cost_estimate=cost(weight.size * 6),
        name="split_heads",
    )(scalars(own), weight)


def join_rows(pieces, own):
    rows, cols = pieces[0].shape
    size = len(pieces)
    if rows % 8:
        stacked = jnp.stack(pieces)
        return stacked[own ^ jnp.arange(size)].reshape(size * rows, cols)

    def kernel(own_ref, *refs):
        out_ref, wide_ref = refs[size], refs[size + 1]
        for other in range(size):
            at = pl.multiple_of((own_ref[0] ^ other) * rows, 8)
            wide_ref[pl.ds(at, rows), :] = refs[other][...].astype(F32)
        out_ref[...] = wide_ref[...].astype(BF16)

    return pl.pallas_call(
        kernel,
        out_shape=jax.ShapeDtypeStruct((size * rows, cols), BF16),
        in_specs=[SCALARS] + [IN_VMEM] * size,
        out_specs=IN_VMEM,
        scratch_shapes=[pltpu.VMEM((size * rows, cols), F32)],
        compiler_params=params(),
        cost_estimate=cost(size * rows * cols * 4),
        name="join_rows",
    )(scalars(own), *pieces)


def split_rows(parts, own):
    size = lax.axis_size("head")
    rows, cols = parts[0].shape[0] // size, parts[0].shape[1]
    if rows % 8:
        total = sum(part.astype(F32) for part in parts).reshape(size, rows, cols)
        total = total[own ^ jnp.arange(size)].astype(BF16)
        return [total[other] for other in range(size)]

    def kernel(own_ref, *refs):
        outs, wide_ref = refs[len(parts) : -1], refs[-1]
        total = refs[0][...].astype(F32)
        for part in refs[1 : len(parts)]:
            total = total + part[...].astype(F32)
        wide_ref[...] = total
        for other in range(size):
            at = pl.multiple_of((own_ref[0] ^ other) * rows, 8)
            outs[other][...] = wide_ref[pl.ds(at, rows), :].astype(BF16)

    return pl.pallas_call(
        kernel,
        out_shape=[jax.ShapeDtypeStruct((rows, cols), BF16)] * size,
        in_specs=[SCALARS] + [IN_VMEM] * len(parts),
        out_specs=[IN_VMEM] * size,
        scratch_shapes=[pltpu.VMEM((size * rows, cols), F32)],
        compiler_params=params(),
        cost_estimate=cost(size * rows * cols * 12),
        name="split_rows",
    )(scalars(own), *parts)


def row_block(rows, most):
    return max(one for one in range(1, rows + 1) if rows % one == 0 and one <= most and (one % 16 == 0 or one == rows))


def split_units(weight, z):
    size = lax.axis_size("ctx")
    count, rows, cols = weight.shape[0], weight.shape[1], weight.shape[2] // size
    block = row_block(rows, 96)

    def kernel(z_ref, in_ref, *refs):
        outs, kept = refs[:size], refs[size]
        for part in range(size):
            for one in range(count):
                kept[part, :, one * cols : (one + 1) * cols] = in_ref[
                    one, :, part * cols : (part + 1) * cols
                ]
        for k in range(size):
            outs[k][...] = kept[lax.rem(z_ref[0] + k, size)].astype(BF16)

    return pl.pallas_call(
        kernel,
        grid=(rows // block,),
        out_shape=[jax.ShapeDtypeStruct((rows, count * cols), BF16)] * size,
        in_specs=[SCALARS, pl.BlockSpec((count, block, size * cols), lambda i: (0, i, 0))],
        out_specs=[pl.BlockSpec((block, count * cols), lambda i: (i, 0))] * size,
        scratch_shapes=[pltpu.VMEM((size, block, count * cols), F32)],
        compiler_params=params(),
        cost_estimate=cost(weight.size * 6),
        name="split_units",
    )(scalars(z), weight)


def adam_units(came, z, weight, first_old, second_old, step_rate):
    size = len(came)
    count = weight.shape[0]
    rows, cols = came[0].shape[0], came[0].shape[1] // count
    block = row_block(rows, 96 // count)

    def kernel(z_ref, *refs):
        pieces, (weight_ref, first_ref, second_ref) = refs[:size], refs[size : size + 3]
        outs, kept = refs[size + 3 : size + 7], refs[size + 7]
        for k in range(size):
            kept[lax.rem(z_ref[0] + (size - k), size)] = pieces[k][...].astype(F32)
        for part in range(size):
            for one in range(count):
                outs[0][one, :, part * cols : (part + 1) * cols] = kept[
                    part, :, one * cols : (one + 1) * cols
                ]
        outs[1][...], outs[2][...], outs[3][...] = adam_step(
            weight_ref[...], first_ref[...], second_ref[...], outs[0][...], step_rate, WEIGHT_DECAY
        )

    whole = pl.BlockSpec((count, block, size * cols), lambda i: (0, i, 0))
    return pl.pallas_call(
        kernel,
        grid=(rows // block,),
        out_shape=[jax.ShapeDtypeStruct(weight.shape, F32)] * 4,
        in_specs=[SCALARS]
        + [pl.BlockSpec((block, count * cols), lambda i: (i, 0))] * size
        + [whole] * 3,
        out_specs=[whole] * 4,
        scratch_shapes=[pltpu.VMEM((size, block, count * cols), F32)],
        compiler_params=params(),
        cost_estimate=cost(weight.size * 30),
        name="adam_units",
    )(scalars(z), *came, weight, first_old, second_old)


def adam_qkv(query_pieces, kv_pieces, own, weight, first_old, second_old):
    size = len(query_pieces)
    query_cols, kv_cols = query_pieces[0].shape[1], kv_pieces[0].shape[1] // 2

    def kernel(own_ref, *refs):
        (weight_ref, first_ref, second_ref), outs = refs[2 * size : 2 * size + 3], refs[2 * size + 3 :]
        grad_ref = outs[0]
        if size > KVH:
            grad_ref[:, QH * HD :] = jnp.zeros_like(grad_ref[:, QH * HD :])
        for other in range(size):
            head = own_ref[0] ^ other
            columns = pl.ds(pl.multiple_of(head * query_cols, HD), query_cols)
            grad_ref[:, columns] = refs[other][...].astype(F32)
            for at in (0, 1):
                start = (QH + at * KVH) * HD + kv_start(head)
                columns = pl.ds(pl.multiple_of(start, HD), kv_cols)
                piece = refs[size + other][:, at * kv_cols : (at + 1) * kv_cols].astype(F32)
                if size > KVH:
                    piece = piece + grad_ref[:, columns]
                grad_ref[:, columns] = piece
        outs[1][...], outs[2][...], outs[3][...] = adam_step(
            weight_ref[...], first_ref[...], second_ref[...], grad_ref[...], RATE_MATRIX, WEIGHT_DECAY
        )

    return pl.pallas_call(
        kernel,
        out_shape=[jax.ShapeDtypeStruct(weight.shape, F32)] * 4,
        in_specs=[SCALARS] + [IN_VMEM] * (2 * size + 3),
        out_specs=[IN_VMEM] * 4,
        compiler_params=params(),
        cost_estimate=cost(weight.size * 30),
        name="adam_qkv",
    )(scalars(own), *query_pieces, *kv_pieces, weight, first_old, second_old)


def matmul(left, right):
    return jnp.dot(left, right, preferred_element_type=F32)


def matmul_nt(left, right):
    return lax.dot_general(left, right, (((1,), (1,)), ((), ())), preferred_element_type=F32)


def matmul_tn(left, right):
    return lax.dot_general(left, right, (((0,), (0,)), ((), ())), preferred_element_type=F32)


def rms_norm(values, gain_row):
    inv_scale = lax.rsqrt(jnp.mean(values * values, axis=-1, keepdims=True) + EPS_NORM)
    return values * inv_scale * (1.0 + gain_row)


def norm_back(values, gain_row, upstream):
    inv_scale = lax.rsqrt(jnp.mean(values * values, axis=-1, keepdims=True) + EPS_NORM)
    unit_rows = values * inv_scale
    scaled = upstream * (1.0 + gain_row)
    result = inv_scale * (scaled - unit_rows * jnp.mean(scaled * unit_rows, axis=-1, keepdims=True))
    return (result, jnp.sum(upstream * unit_rows, axis=0))


def rope_tables(position, half_dim):
    freq_table = ROPE_BASE ** (-(jnp.arange(half_dim, dtype=F32) * 2.0 / (2 * half_dim)))
    angle_table = position.astype(F32)[:, None] * freq_table[None, :]
    return (jnp.cos(angle_table), jnp.sin(angle_table))


def rope_turn(values, cosine, sine_table):
    half_dim = values.shape[-1] // 2
    lead_half = values[..., :half_dim]
    tail_half = values[..., half_dim:]
    return jnp.concatenate(
        [lead_half * cosine - tail_half * sine_table, tail_half * cosine + lead_half * sine_table],
        axis=-1,
    )


def rope_back(grad_rows, cosine, sine_table):
    return rope_turn(grad_rows, cosine, -sine_table)


def gated_unit(gate_in, up_in):
    return jax.nn.gelu(gate_in, approximate=True) * up_in


def adam_step(weight, first_old, second_old, gradient, step_rate, decay_rate):
    first_new = BETA_ONE * first_old + (1.0 - BETA_ONE) * gradient
    second_new = BETA_TWO * second_old + (1.0 - BETA_TWO) * gradient * gradient
    first_hat = first_new / (1.0 - BETA_ONE**STEP)
    second_hat = second_new / (1.0 - BETA_TWO**STEP)
    weight_new = weight - step_rate * (
        first_hat / (jnp.sqrt(second_hat) + EPS_ADAM) + decay_rate * weight
    )
    return (first_new, second_new, weight_new)


def block_weights(queries, keys, query_pos, key_pos):
    scores = jnp.einsum("kqd,krd->kqr", queries, keys, preferred_element_type=F32)
    unit = jnp.tanh(scores / SOFT_CAP)
    allowed = key_pos[None, None, :] <= query_pos[None, :, None]
    return (unit, jnp.where(allowed, jnp.exp(SOFT_CAP * unit), 0.0))


def block_forward(queries, keys, values, query_pos, key_pos):
    unused, weights = block_weights(queries, keys, query_pos, key_pos)
    return (
        jnp.sum(weights, axis=-1, keepdims=True),
        jnp.einsum("kqr,krd->kqd", weights.astype(BF16), values, preferred_element_type=F32),
    )


def block_backward(queries, keys, values, query_pos, key_pos, grad_summed, delta):
    unit, weights = block_weights(queries, keys, query_pos, key_pos)
    grad_weights = jnp.einsum("kqd,krd->kqr", grad_summed, values, preferred_element_type=F32)
    grad_scores = (weights * (grad_weights - delta) * (1.0 - unit * unit)).astype(BF16)
    return (
        jnp.einsum("kqr,krd->kqd", grad_scores, keys, preferred_element_type=F32),
        jnp.einsum("kqr,kqd->krd", grad_scores, queries, preferred_element_type=F32),
        jnp.einsum("kqr,kqd->krd", weights.astype(BF16), grad_summed, preferred_element_type=F32),
    )


def shards(
    tokens,
    positions,
    cotangent,
    qkv_weight,
    qkv_first,
    qkv_second,
    out_weight,
    out_first,
    out_second,
    gate_up,
    gate_up_first,
    gate_up_second,
    down_weight,
    down_first,
    down_second,
    gains,
    gains_first,
    gains_second,
):
    size_x, size_z, size_h = lax.axis_size("fsdp"), lax.axis_size("ctx"), lax.axis_size("head")
    z, own_h = lax.axis_index("ctx"), lax.axis_index("head")
    tok_rows, width = tokens.shape
    block_rows = tok_rows * size_h
    order = head_order()
    copies = max(1, size_h // KVH)
    kv_local = KVH * copies // size_h
    query_local = QH // size_h
    group = query_local // kv_local
    query_scale = 1.0 / math.sqrt(HD)
    query_cols, kv_cols = query_local * HD, kv_local * HD

    def positions_of(block):
        rows = lax.dynamic_slice_in_dim(positions, block * block_rows, block_rows)
        return jnp.concatenate(
            [lax.dynamic_slice_in_dim(rows, (own_h ^ one) * tok_rows, tok_rows) for one in order]
        )

    lines = Lines()
    unit_order = [k for k in far_first(size_z) if k]
    far_k = unit_order[0]

    pieces = head_exchange(lines, split_heads(qkv_weight, own_h))
    qkv_piece = join_rows(pieces, own_h)
    qkv_rows, local_cols = qkv_weight.shape[0], qkv_piece.shape[1]
    more_tokens = [tokens] + swap_top(lines, tokens) if size_h > 1 else [tokens]
    qkv_parts = spread_ctx(lines, qkv_piece, swap_fsdp)
    qkv_full = put_pieces(qkv_parts).reshape(width, local_cols)
    gain_rows = gather_gains(after(gains, qkv_piece))

    out_rows = out_weight.shape[0]
    out_groups = size_x * size_z // size_h
    out_low = after(out_weight, qkv_piece).astype(BF16)
    out_parts = spread_ctx(lines, out_low, swap_fsdp)
    out_own = put_pieces(out_parts).reshape(size_h, out_groups, out_rows, width)
    out_sets = head_exchange(lines, pick_pieces(out_own, [own_h ^ i for i in range(size_h)]))
    out_full = place(out_sets, [own_h ^ i for i in range(size_h)])
    out_full = jnp.transpose(out_full, (1, 0, 2, 3)).reshape(query_cols, width)

    ff_rows = gate_up.shape[1]
    ff_cols = gate_up.shape[2] // size_z
    down_turned = down_weight.T[None]
    gate_up_low = split_units(after(gate_up, qkv_piece), z)
    down_low = split_units(after(down_turned, qkv_piece), z)

    def unit_part(k, low):
        one = send_ctx(lines, low[k], k) if k else low[0]
        source = lambda z: lax.rem(z - k + size_z, size_z)
        return ([one] + swap_fsdp(lines, one), source, lambda z: z >= 0)

    gate_up_parts = [unit_part(k, gate_up_low) for k in (0, far_k)]

    block_tokens = head_gather(lines, jnp.concatenate(more_tokens), head_bits()[1:]).astype(F32)
    inputs = tokens.astype(F32)
    first_normed = rms_norm(block_tokens, gain_rows[0]).astype(BF16)
    projected = matmul(first_normed, qkv_full)
    block_pos = positions_of(z)
    cosine, sine_table = rope_tables(block_pos, HD // 2)

    def heads_of(values, count):
        return jnp.transpose(values.reshape(block_rows, count, HD), (1, 0, 2))

    queries = heads_of(projected[:, :query_cols], query_local)
    queries = (rope_turn(queries, cosine, sine_table) * query_scale).astype(BF16)
    queries = queries.reshape(kv_local, group * block_rows, HD)
    own_keys = heads_of(projected[:, query_cols : query_cols + kv_cols], kv_local)
    own_keys = rope_turn(own_keys, cosine, sine_table).astype(BF16)
    own_values = heads_of(projected[:, query_cols + kv_cols :], kv_local).astype(BF16)
    query_pos = jnp.tile(block_pos, group)
    own_kv = jnp.stack([own_keys, own_values])
    kv_slots = ctx_slots(lines, own_kv)
    gate_up_parts += [unit_part(k, gate_up_low) for k in unit_order[1:]]
    pos_slots = [positions_of(lax.rem(z + k, size_z)) for k in range(size_z)]
    exp_total = 0.0
    summed = 0.0
    for kv_slot, key_pos in zip(kv_slots, pos_slots):
        total_part, summed_part = block_forward(
            queries, kv_slot[0], kv_slot[1], query_pos, key_pos
        )
        exp_total = exp_total + total_part
        summed = summed + summed_part
    attended = summed / exp_total

    def rows_of(heads):
        heads = heads.reshape(-1, block_rows, HD)
        return jnp.transpose(heads, (1, 0, 2)).reshape(block_rows, -1)

    attended_low = rows_of(attended.astype(BF16))
    attn_out = head_reduce(lines, matmul(attended_low, out_full).astype(BF16))
    middle = inputs + rms_norm(attn_out, gain_rows[1])
    second_normed = rms_norm(middle, gain_rows[2]).astype(BF16)

    def all_slots(rows):
        if size_h < 2:
            return ctx_slots(lines, rows)
        slots = ctx_slots(lines, rows, swap_top, jnp.concatenate)
        return [head_gather(lines, one, head_bits()[1:]) for one in slots]

    def sum_slots(parts):
        return sum_ctx_slots(lines, lambda k: head_reduce(lines, parts[k]))

    normed_slots = all_slots(second_normed)
    down_parts = [unit_part(k, down_low) for k in [0] + unit_order]
    gate_up_full = put_pieces(gate_up_parts).reshape(width, 2 * ff_cols)
    down_full = put_pieces(down_parts).reshape(width, ff_cols)
    act_slots = [matmul(rows, gate_up_full) for rows in normed_slots]
    hidden_slots = [
        gated_unit(act[:, :ff_cols], act[:, ff_cols:]).astype(BF16) for act in act_slots
    ]
    ffn_out = sum_slots([matmul_nt(hidden, down_full).astype(BF16) for hidden in hidden_slots])
    mixed_out = (middle + rms_norm(ffn_out, gain_rows[3])).astype(BF16)

    upstream = cotangent.astype(F32)
    grad_ffn, gain_grad_ffn = norm_back(ffn_out, gain_rows[3], upstream)
    grad_slots = all_slots(grad_ffn.astype(BF16))

    def units_back(term, cols):
        sums = sum_over_fsdp(
            lines, term.reshape(size_x * size_z, ff_rows, cols), unit_order + [0]
        )
        return {k: one if k == 0 else one.astype(BF16) for k, one in sums.items()}

    down_term = matmul_tn(jnp.concatenate(grad_slots), jnp.concatenate(hidden_slots)).astype(BF16)
    down_back = units_back(down_term, ff_cols)
    for k in unit_order:
        down_back[k] = send_ctx(lines, down_back[k], k)
    grad_act_slots = []
    for rows, act in zip(grad_slots, act_slots):
        grad_hidden = matmul(rows, down_full)
        unit_out, unit_back = jax.vjp(gated_unit, act[:, :ff_cols], act[:, ff_cols:])
        grad_act_slots.append(jnp.concatenate(unit_back(grad_hidden), axis=1).astype(BF16))
    grad_second_parts = [matmul_nt(rows, gate_up_full).astype(BF16) for rows in grad_act_slots]
    gate_up_term = matmul_tn(jnp.concatenate(normed_slots), jnp.concatenate(grad_act_slots))
    gate_up_term = gate_up_term.astype(BF16)
    grad_second_parts[0] = after(grad_second_parts[0], gate_up_term)
    grad_second = sum_slots(grad_second_parts)
    gate_up_back = units_back(gate_up_term, 2 * ff_cols)
    gate_up_back[far_k] = send_ctx(lines, gate_up_back[far_k], far_k)

    grad_middle_part, gain_grad_middle = norm_back(middle, gain_rows[2], grad_second)
    grad_middle = upstream + grad_middle_part
    grad_attn, gain_grad_attn = norm_back(attn_out, gain_rows[1], grad_middle)
    block_grad_attn = head_gather(lines, grad_attn.astype(BF16))
    out_term = matmul_tn(attended_low, block_grad_attn).astype(BF16)
    out_term = jnp.transpose(
        out_term.reshape(out_groups, size_h, out_rows, width), (1, 0, 2, 3)
    )
    grad_attended = matmul_nt(block_grad_attn, out_full).astype(BF16)
    grad_attended = heads_of(grad_attended, query_local).astype(F32)
    grad_attended = grad_attended.reshape(kv_local, group * block_rows, HD)
    row_delta = jnp.sum(grad_attended * attended, axis=-1, keepdims=True)
    delta = row_delta / exp_total
    grad_summed = (grad_attended / exp_total).astype(BF16)
    grad_query = 0.0
    kv_parts = {}
    for k in ctx_order():
        query_part, key_part, value_part = block_backward(
            queries, kv_slots[k][0], kv_slots[k][1], query_pos, pos_slots[k], grad_summed, delta
        )
        grad_query = grad_query + query_part
        kv_parts[k] = jnp.stack([key_part, value_part])
    grad_kv = sum_ctx_slots(lines, lambda k: kv_parts[k])
    for k in unit_order[1:]:
        gate_up_back[k] = send_ctx(lines, gate_up_back[k], k)
    out_sets = head_exchange(lines, pick_pieces(out_term, [own_h ^ i for i in range(size_h)]))
    out_term = place(out_sets, [own_h ^ i for i in range(size_h)])

    grad_query = grad_query.astype(BF16).astype(F32).reshape(query_local, block_rows, HD)
    query_proj = rows_of(rope_back(grad_query, cosine, sine_table) * query_scale).astype(BF16)
    query_term = matmul_tn(first_normed, query_proj).astype(BF16)
    query_sums = sum_over_fsdp(
        lines, query_term.reshape(size_x * size_z, size_h * qkv_rows, query_cols), ctx_order()
    )
    query_sum = sum_ctx_slots(lines, lambda k: query_sums[k])
    grad_kv = grad_kv.astype(BF16).astype(F32)
    kv_proj = jnp.concatenate(
        [rows_of(rope_back(grad_kv[0], cosine, sine_table)), rows_of(grad_kv[1])], axis=1
    ).astype(BF16)
    kv_term = matmul_tn(first_normed, kv_proj).astype(BF16)
    kv_sums = sum_over_fsdp(
        lines, kv_term.reshape(size_x * size_z, size_h * qkv_rows, 2 * kv_cols), ctx_order()
    )
    kv_sum = sum_ctx_slots(lines, lambda k: kv_sums[k])
    grad_proj = jnp.concatenate([query_proj, kv_proj], axis=1)
    grad_first = head_reduce(lines, matmul_nt(grad_proj, qkv_full).astype(BF16))
    grad_input_part, gain_grad_input = norm_back(inputs, gain_rows[0], grad_first)
    tokens_grad = (grad_middle + grad_input_part).astype(BF16)

    query_pieces = head_exchange(lines, split_rows([query_sum], own_h))
    kv_pieces = head_exchange(lines, split_rows([kv_sum], own_h))
    out_sums = sum_over_fsdp(
        lines, out_term.reshape(size_x * size_z, out_rows, width), ctx_order()
    )
    out_grad = sum_ctx_slots(lines, lambda k: out_sums[k])
    gains_grad = scatter_gains(
        jnp.stack([gain_grad_input, gain_grad_attn, gain_grad_middle, gain_grad_ffn])
    )

    qkv_grad, qkv_first_new, qkv_second_new, qkv_new = adam_qkv(
        query_pieces, kv_pieces, own_h, qkv_weight, qkv_first, qkv_second
    )
    out_first_new, out_second_new, out_new = adam_step(
        out_weight, out_first, out_second, out_grad, RATE_MATRIX, WEIGHT_DECAY
    )
    gate_up_grad, gate_up_first_new, gate_up_second_new, gate_up_new = adam_units(
        [gate_up_back[k] for k in range(size_z)], z, gate_up, gate_up_first, gate_up_second, RATE_MATRIX
    )
    down_outs = adam_units(
        [down_back[k] for k in range(size_z)],
        z,
        down_turned,
        down_first.T[None],
        down_second.T[None],
        RATE_DOWN,
    )
    down_grad, down_first_new, down_second_new, down_new = [one[0].T for one in down_outs]
    gains_first_new, gains_second_new, gains_new = adam_step(
        gains, gains_first, gains_second, gains_grad, RATE_GAIN, 0.0
    )
    return (
        mixed_out,
        tokens_grad,
        qkv_grad,
        qkv_first_new,
        qkv_second_new,
        qkv_new,
        out_grad,
        out_first_new,
        out_second_new,
        out_new,
        gate_up_grad,
        gate_up_first_new,
        gate_up_second_new,
        gate_up_new,
        down_grad,
        down_first_new,
        down_second_new,
        down_new,
        gains_grad,
        gains_first_new,
        gains_second_new,
        gains_new,
    )


TOKEN_SPEC = P(("fsdp", "ctx", "head"), None)
GATE_UP_SPEC = P(None, ("fsdp", "ctx"), "head")
DOWN_SPEC = P("head", ("fsdp", "ctx"))


def solution(mesh):
    in_specs = (
        (TOKEN_SPEC, P("fsdp"))
        + (TOKEN_SPEC,) * 7
        + (GATE_UP_SPEC,) * 3
        + (DOWN_SPEC,) * 3
        + (TOKEN_SPEC,) * 3
    )
    out_specs = (
        (TOKEN_SPEC,) * 10 + (GATE_UP_SPEC,) * 4 + (DOWN_SPEC,) * 4 + (TOKEN_SPEC,) * 4
    )
    return jax.shard_map(shards, mesh=mesh, in_specs=in_specs, out_specs=out_specs, check_vma=False)
```

```python
import functools
import math

import jax
import jax.numpy as jnp
from jax import lax
from jax.experimental import pallas as pl
from jax.experimental.pallas import tpu as pltpu
from jax.sharding import PartitionSpec as P

QH = 8
KVH = 4
HD = 256
STEP = 10


SOFT_CAP = 50.0
EPS_NORM = 1e-06
ROPE_BASE = 10000.0
BETA_ONE = 0.9
BETA_TWO = 0.95
EPS_ADAM = 1e-08
RATE_MATRIX = 0.05
RATE_DOWN = 0.025
RATE_GAIN = 0.5
WEIGHT_DECAY = 0.1

BF16 = jnp.bfloat16
F32 = jnp.float32


def after(values, *others):
    return lax.optimization_barrier((values,) + others)[0]


class Line:
    def __init__(self, depth):
        self.depth = depth
        self.came = []

    def send(self, sendings):
        values = tuple(one for one, _, _ in sendings)
        if len(self.came) >= self.depth:
            values = after(values, *self.came[-self.depth])
        results = [
            lax.ppermute(one, axes, pairs) for one, (_, axes, pairs) in zip(values, sendings)
        ]
        self.came.append(tuple(results))
        return results


class Lines:
    def __init__(self):
        self.fsdp, self.ctx, self.head, self.pair = Line(2), Line(2), Line(2), Line(2)


DEPTH = 2


def ring_pairs(size, step):
    return [(i, (i + step) % size) for i in range(size)]


def swap_bit(lines, values, bit):
    size = lax.axis_size("head")
    pairs = [(i, i ^ bit) for i in range(size)]
    if bit == 1 and size > 2:
        return lax.ppermute(values, "head", pairs)
    return lines.head.send([(values, "head", pairs)])[0]


def send_ctx(lines, values, step):
    return lines.ctx.send([(values, "ctx", ring_pairs(lax.axis_size("ctx"), step))])[0]


def swap_ctx(lines, values, other):
    pairs = [(z, z ^ other) for z in range(lax.axis_size("ctx"))]
    line = lines.pair if other == 1 else lines.ctx
    return line.send([(values, "ctx", pairs)])[0]


def unit_part(lines, one, other):
    return ([one] + swap_fsdp(lines, one), lambda z: z ^ other, lambda z: z >= 0)


def units_back(lines, pieces):
    size_x, size_z = lax.axis_size("fsdp"), lax.axis_size("ctx")
    x, z = lax.axis_index("fsdp"), lax.axis_index("ctx")
    order = [k ^ 1 for k in range(2, size_z)] + [1, 0]
    chosen = [(k, step) for k in order for step in range(size_x)]
    picked = pick_pieces(
        pieces, [lax.rem(x + step, size_x) * size_z + (z ^ k) for k, step in chosen]
    )
    picked = dict(zip(chosen, picked))
    sums = {}
    for k in order:
        sums[k] = picked[k, 0].astype(F32)
        for step in range(1, size_x):
            pairs = ring_pairs(size_x, step)
            came = lines.fsdp.send([(picked[k, step], "fsdp", pairs)])[0]
            sums[k] = sums[k] + came.astype(F32)
    return sums


def units_sent(lines, sums, low, *others):
    total = sums[low]
    for other in range(2, lax.axis_size("ctx"), 2):
        one = sums[other ^ low].astype(BF16)
        one = swap_ctx(lines, after(one, *others) if others else one, other)
        total = total + one.astype(F32)
    return swap_ctx(lines, total.astype(BF16), 1) if low else total


def swap_fsdp(lines, values, valid=lambda z: True):
    size_x, size_z = lax.axis_size("fsdp"), lax.axis_size("ctx")
    return [
        lines.fsdp.send(
            [
                (
                    values,
                    ("fsdp", "ctx"),
                    [
                        (x * size_z + z, (x + step) % size_x * size_z + z)
                        for x in range(size_x)
                        for z in range(size_z)
                        if valid(z)
                    ],
                )
            ]
        )[0]
        for step in range(1, size_x)
    ]


def swap_top(lines, values, valid=lambda z: True):
    size_z, size_h = lax.axis_size("ctx"), lax.axis_size("head")
    pairs = [
        (z * size_h + h, z * size_h + (h ^ (size_h // 2)))
        for z in range(size_z)
        for h in range(size_h)
        if valid(z)
    ]
    return lines.head.send([(values, ("ctx", "head"), pairs)])


def head_bits():
    bits = []
    bit = lax.axis_size("head") // 2
    while bit:
        bits.append(bit)
        bit //= 2
    return bits


def head_order():
    order = [0]
    for bit in head_bits():
        order = order + [one ^ bit for one in order]
    return order


def head_gather(lines, rows, bits=None):
    for bit in head_bits() if bits is None else bits:
        rows = jnp.concatenate([rows, swap_bit(lines, rows, bit)], axis=0)
    return rows


def head_reduce(lines, part):
    for bit in reversed(head_bits()):
        half = part.shape[0] // 2
        came = swap_bit(lines, part[half:].astype(BF16), bit)
        part = part[:half].astype(F32) + came.astype(F32)
    return part


def head_exchange(lines, pieces):
    return [pieces[0]] + [swap_bit(lines, pieces[i], i) for i in range(1, len(pieces))]


AHEAD, BACK = [(0, 1), (1, 2), (2, 3)], [(1, 0), (2, 1), (3, 2)]
TWO, ENDS = [(0, 2), (1, 3), (2, 0), (3, 1)], [(2, 3), (1, 0)]
FAR = [(0, 1), (3, 2)]


def spread_ctx(lines, own, swaps):
    size = lax.axis_size("ctx")
    always = lambda z: z >= 0
    parts = [([own] + swaps(lines, own), lambda z: z, always)]
    if size != 4:
        for k in range(1, size):
            one = send_ctx(lines, own, k)
            source = lambda z, k=k: (z - k + size) % size
            parts.append(([one] + swaps(lines, one), source, always))
        return parts
    not_first, not_last, at_end = lambda z: z >= 1, lambda z: z <= 2, lambda z: z % 3 == 0
    ahead, back = lines.ctx.send([(own, "ctx", AHEAD), (own, "ctx", BACK)])
    two = lines.ctx.send([(after(own, ahead, back), "ctx", TWO)])[0]
    parts.append(([ahead] + swaps(lines, ahead, not_first), lambda z: z - 1, not_first))
    parts.append(([back] + swaps(lines, back, not_last), lambda z: z + 1, not_last))
    two = after(two, *parts[1][0][1:])
    ends = lines.ctx.send([(two, "ctx", ENDS)])[0]
    parts.append(([two] + swaps(lines, two), lambda z: z ^ 2, always))
    parts.append(([ends] + swaps(lines, ends, at_end), lambda z: 3 - z, at_end))
    return parts


def put_pieces(parts):
    size_x, size_z = lax.axis_size("fsdp"), lax.axis_size("ctx")
    x, z = lax.axis_index("fsdp"), lax.axis_index("ctx")
    arrays, places = [], []
    for by_step, source, valid in parts:
        for step, one in enumerate(by_step):
            at = lax.rem(x - step + size_x, size_x) * size_z + source(z)
            arrays.append(one)
            places.append(jnp.where(valid(z), at, -1))
    return place(arrays, places, size_x * size_z)


def ctx_slots(lines, values, swaps=lambda lines, values, valid=None: [], join=lambda arrays: arrays[0]):
    size = lax.axis_size("ctx")
    arrays = [join(by_step) for by_step, _, _ in spread_ctx(lines, values, swaps)]
    if size != 4:
        return [arrays[0]] + [arrays[size - k] for k in range(1, size)]
    z = lax.axis_index("ctx")
    own, ahead, back, two, ends = arrays
    return [own, jnp.where(z == 3, ends, back), two, jnp.where(z == 0, ends, ahead)]


def sum_ctx_slots(lines, part_of):
    size = lax.axis_size("ctx")
    z = lax.axis_index("ctx")
    if size != 4:
        total = 0.0
        for k in ctx_order():
            part = part_of(k)
            total = total + (send_ctx(lines, part.astype(BF16), k).astype(F32) if k else part)
        return total
    part_one = part_of(1).astype(BF16)
    part_three = part_of(3).astype(BF16)
    far = lines.ctx.send([(jnp.where(z == 0, part_three, part_one), "ctx", FAR)])[0]
    ahead, back = lines.ctx.send([(part_one, "ctx", AHEAD), (part_three, "ctx", BACK)])
    part_two = part_of(2).astype(F32) + far.astype(F32)
    two = lines.ctx.send([(part_two.astype(BF16), "ctx", TWO)])[0]
    return part_of(0).astype(F32) + ahead.astype(F32) + back.astype(F32) + two.astype(F32)


def far_first(size):
    return sorted(range(size), key=lambda k: -min(k, size - k))


def ctx_order():
    size = lax.axis_size("ctx")
    return [1, 3, 2, 0] if size == 4 else far_first(size)


def sum_over_fsdp(lines, pieces, order):
    size_x, size_z = lax.axis_size("fsdp"), lax.axis_size("ctx")
    x, z = lax.axis_index("fsdp"), lax.axis_index("ctx")
    chosen = [(k, step) for k in order for step in range(size_x)]
    picked = pick_pieces(
        pieces,
        [lax.rem(x + step, size_x) * size_z + lax.rem(z + k, size_z) for k, step in chosen],
    )
    picked = dict(zip(chosen, picked))
    sums = {}
    for k in order:
        total = picked[k, 0].astype(F32)
        for step in range(1, size_x):
            pairs = ring_pairs(size_x, step)
            total = total + lines.fsdp.send([(picked[k, step], "fsdp", pairs)])[0].astype(F32)
        sums[k] = total
    return sums


def exchange_all(pieces):
    return lax.all_to_all(
        pieces, ("fsdp", "ctx", "head"), split_axis=0, concat_axis=0, tiled=True
    )


def device_count():
    return lax.axis_size("fsdp") * lax.axis_size("ctx") * lax.axis_size("head")


def gather_gains(gains):
    rows = exchange_all(jnp.broadcast_to(gains.astype(BF16).T[None], (device_count(),) + gains.shape[::-1]))
    return jnp.transpose(rows, (1, 0, 2)).reshape(gains.shape[1], -1).astype(F32)


def scatter_gains(rows):
    pieces = jnp.transpose(rows.reshape(rows.shape[0], device_count(), -1), (1, 0, 2))
    return jnp.sum(exchange_all(pieces), axis=0).T


ANYWHERE = pl.BlockSpec(memory_space=pl.ANY)
SCALARS = pl.BlockSpec(memory_space=pltpu.SMEM)
IN_VMEM = pl.BlockSpec(memory_space=pltpu.VMEM)
VMEM_LIMIT = 48 * 1024 * 1024


def scalars(*values):
    return jnp.stack([jnp.asarray(one, jnp.int32) for one in values])


def cost(byte_count, flops=0):
    return pl.CostEstimate(flops=flops, bytes_accessed=byte_count, transcendentals=0)


def params():
    return pltpu.CompilerParams(vmem_limit_bytes=VMEM_LIMIT)


def place(pieces, places, total=None):
    count = len(pieces)
    shape = (total or count,) + pieces[0].shape

    def kernel(places_ref, *refs):
        out_ref, sems = refs[count], refs[count + 1]

        def each(act):
            for i in range(count):
                copy = pltpu.make_async_copy(
                    refs[i], out_ref.at[jnp.maximum(places_ref[i], 0)], sems.at[i]
                )
                pl.when(places_ref[i] >= 0)(functools.partial(act, copy))

        each(lambda copy: copy.start())
        each(lambda copy: copy.wait())

    return pl.pallas_call(
        kernel,
        out_shape=jax.ShapeDtypeStruct(shape, pieces[0].dtype),
        in_specs=[SCALARS] + [ANYWHERE] * count,
        out_specs=IN_VMEM,
        scratch_shapes=[pltpu.SemaphoreType.DMA((count,))],
        compiler_params=params(),
        cost_estimate=cost(2 * math.prod(shape) * pieces[0].dtype.itemsize),
        name="place",
    )(scalars(*places), *pieces)


def pick_pieces(stacked, places):
    count = len(places)
    shape = stacked.shape[1:]

    def kernel(places_ref, in_ref, *refs):
        sems = refs[count]
        copies = [
            pltpu.make_async_copy(in_ref.at[places_ref[i]], refs[i], sems.at[i])
            for i in range(count)
        ]
        for copy in copies:
            copy.start()
        for copy in copies:
            copy.wait()

    return pl.pallas_call(
        kernel,
        out_shape=[jax.ShapeDtypeStruct(shape, stacked.dtype)] * count,
        in_specs=[SCALARS, IN_VMEM],
        out_specs=[ANYWHERE] * count,
        scratch_shapes=[pltpu.SemaphoreType.DMA((count,))],
        compiler_params=params(),
        cost_estimate=cost(2 * count * math.prod(shape) * stacked.dtype.itemsize),
        name="pick_pieces",
    )(scalars(*places), stacked)


def kv_start(head):
    return lax.div(head * KVH, lax.axis_size("head")) * HD


def split_heads(weight, own):
    rows = weight.shape[0]
    size = lax.axis_size("head")
    query_cols, kv_cols = QH * HD // size, max(1, KVH // size) * HD
    local_cols = query_cols + 2 * kv_cols

    def kernel(own_ref, weight_ref, *outs):
        for other in range(size):
            head = own_ref[0] ^ other
            starts = (head * query_cols, QH * HD + kv_start(head), (QH + KVH) * HD + kv_start(head))
            at = 0
            for start, count in zip(starts, (query_cols, kv_cols, kv_cols)):
                columns = pl.ds(pl.multiple_of(start, HD), count)
                outs[other][:, at : at + count] = weight_ref[:, columns].astype(BF16)
                at += count

    return pl.pallas_call(
        kernel,
        out_shape=[jax.ShapeDtypeStruct((rows, local_cols), BF16)] * size,
        in_specs=[SCALARS, IN_VMEM],
        out_specs=[IN_VMEM] * size,
        compiler_params=params(),
        cost_estimate=cost(weight.size * 6),
        name="split_heads",
    )(scalars(own), weight)


def join_rows(pieces, own):
    rows, cols = pieces[0].shape
    size = len(pieces)
    if rows % 8:
        stacked = jnp.stack(pieces)
        return stacked[own ^ jnp.arange(size)].reshape(size * rows, cols)

    def kernel(own_ref, *refs):
        out_ref, wide_ref = refs[size], refs[size + 1]
        for other in range(size):
            at = pl.multiple_of((own_ref[0] ^ other) * rows, 8)
            wide_ref[pl.ds(at, rows), :] = refs[other][...].astype(F32)
        out_ref[...] = wide_ref[...].astype(BF16)

    return pl.pallas_call(
        kernel,
        out_shape=jax.ShapeDtypeStruct((size * rows, cols), BF16),
        in_specs=[SCALARS] + [IN_VMEM] * size,
        out_specs=IN_VMEM,
        scratch_shapes=[pltpu.VMEM((size * rows, cols), F32)],
        compiler_params=params(),
        cost_estimate=cost(size * rows * cols * 4),
        name="join_rows",
    )(scalars(own), *pieces)


def split_rows(parts, own):
    size = lax.axis_size("head")
    rows, cols = parts[0].shape[0] // size, parts[0].shape[1]
    if rows % 8:
        total = sum(part.astype(F32) for part in parts).reshape(size, rows, cols)
        total = total[own ^ jnp.arange(size)].astype(BF16)
        return [total[other] for other in range(size)]

    def kernel(own_ref, *refs):
        outs, wide_ref = refs[len(parts) : -1], refs[-1]
        total = refs[0][...].astype(F32)
        for part in refs[1 : len(parts)]:
            total = total + part[...].astype(F32)
        wide_ref[...] = total
        for other in range(size):
            at = pl.multiple_of((own_ref[0] ^ other) * rows, 8)
            outs[other][...] = wide_ref[pl.ds(at, rows), :].astype(BF16)

    return pl.pallas_call(
        kernel,
        out_shape=[jax.ShapeDtypeStruct((rows, cols), BF16)] * size,
        in_specs=[SCALARS] + [IN_VMEM] * len(parts),
        out_specs=[IN_VMEM] * size,
        scratch_shapes=[pltpu.VMEM((size * rows, cols), F32)],
        compiler_params=params(),
        cost_estimate=cost(size * rows * cols * 12),
        name="split_rows",
    )(scalars(own), *parts)


def row_block(rows, most):
    return max(one for one in range(1, rows + 1) if rows % one == 0 and one <= most and (one % 16 == 0 or one == rows))


def split_units(weight, own, size):
    count, rows, cols = weight.shape[0], weight.shape[1], weight.shape[2] // size
    block = row_block(rows, 96)

    def kernel(own_ref, in_ref, *refs):
        outs, kept = refs[:size], refs[size]
        for part in range(size):
            for one in range(count):
                kept[part, :, one * cols : (one + 1) * cols] = in_ref[
                    one, :, part * cols : (part + 1) * cols
                ]
        for k in range(size):
            outs[k][...] = kept[own_ref[0] ^ k].astype(BF16)

    return pl.pallas_call(
        kernel,
        grid=(rows // block,),
        out_shape=[jax.ShapeDtypeStruct((rows, count * cols), BF16)] * size,
        in_specs=[SCALARS, pl.BlockSpec((count, block, size * cols), lambda i: (0, i, 0))],
        out_specs=[pl.BlockSpec((block, count * cols), lambda i: (i, 0))] * size,
        scratch_shapes=[pltpu.VMEM((size, block, count * cols), F32)],
        compiler_params=params(),
        cost_estimate=cost(weight.size * 6),
        name="split_units",
    )(scalars(own), weight)


def adam_units(came, own, weight, first_old, second_old, step_rate):
    size = len(came)
    count = weight.shape[0]
    rows, cols = came[0].shape[0], came[0].shape[1] // count
    block = row_block(rows, 96 // count)

    def kernel(own_ref, *refs):
        pieces, (weight_ref, first_ref, second_ref) = refs[:size], refs[size : size + 3]
        outs, kept = refs[size + 3 : size + 7], refs[size + 7]
        for k in range(size):
            kept[own_ref[0] ^ k] = pieces[k][...].astype(F32)
        for part in range(size):
            for one in range(count):
                outs[0][one, :, part * cols : (part + 1) * cols] = kept[
                    part, :, one * cols : (one + 1) * cols
                ]
        outs[1][...], outs[2][...], outs[3][...] = adam_step(
            weight_ref[...], first_ref[...], second_ref[...], outs[0][...], step_rate, WEIGHT_DECAY
        )

    whole = pl.BlockSpec((count, block, size * cols), lambda i: (0, i, 0))
    return pl.pallas_call(
        kernel,
        grid=(rows // block,),
        out_shape=[jax.ShapeDtypeStruct(weight.shape, F32)] * 4,
        in_specs=[SCALARS]
        + [pl.BlockSpec((block, count * cols), lambda i: (i, 0))] * size
        + [whole] * 3,
        out_specs=[whole] * 4,
        scratch_shapes=[pltpu.VMEM((size, block, count * cols), F32)],
        compiler_params=params(),
        cost_estimate=cost(weight.size * 30),
        name="adam_units",
    )(scalars(own), *came, weight, first_old, second_old)


def adam_qkv(query_pieces, kv_pieces, own, weight, first_old, second_old):
    size = len(query_pieces)
    query_cols, kv_cols = query_pieces[0].shape[1], kv_pieces[0].shape[1] // 2

    def kernel(own_ref, *refs):
        (weight_ref, first_ref, second_ref), outs = refs[2 * size : 2 * size + 3], refs[2 * size + 3 :]
        grad_ref = outs[0]
        if size > KVH:
            grad_ref[:, QH * HD :] = jnp.zeros_like(grad_ref[:, QH * HD :])
        for other in range(size):
            head = own_ref[0] ^ other
            columns = pl.ds(pl.multiple_of(head * query_cols, HD), query_cols)
            grad_ref[:, columns] = refs[other][...].astype(F32)
            for at in (0, 1):
                start = (QH + at * KVH) * HD + kv_start(head)
                columns = pl.ds(pl.multiple_of(start, HD), kv_cols)
                piece = refs[size + other][:, at * kv_cols : (at + 1) * kv_cols].astype(F32)
                if size > KVH:
                    piece = piece + grad_ref[:, columns]
                grad_ref[:, columns] = piece
        outs[1][...], outs[2][...], outs[3][...] = adam_step(
            weight_ref[...], first_ref[...], second_ref[...], grad_ref[...], RATE_MATRIX, WEIGHT_DECAY
        )

    return pl.pallas_call(
        kernel,
        out_shape=[jax.ShapeDtypeStruct(weight.shape, F32)] * 4,
        in_specs=[SCALARS] + [IN_VMEM] * (2 * size + 3),
        out_specs=[IN_VMEM] * 4,
        compiler_params=params(),
        cost_estimate=cost(weight.size * 30),
        name="adam_qkv",
    )(scalars(own), *query_pieces, *kv_pieces, weight, first_old, second_old)


def matmul(left, right):
    return jnp.dot(left, right, preferred_element_type=F32)


def matmul_nt(left, right):
    return lax.dot_general(left, right, (((1,), (1,)), ((), ())), preferred_element_type=F32)


def matmul_tn(left, right):
    return lax.dot_general(left, right, (((0,), (0,)), ((), ())), preferred_element_type=F32)


def rms_norm(values, gain_row):
    inv_scale = lax.rsqrt(jnp.mean(values * values, axis=-1, keepdims=True) + EPS_NORM)
    return values * inv_scale * (1.0 + gain_row)


def norm_back(values, gain_row, upstream):
    inv_scale = lax.rsqrt(jnp.mean(values * values, axis=-1, keepdims=True) + EPS_NORM)
    unit_rows = values * inv_scale
    scaled = upstream * (1.0 + gain_row)
    result = inv_scale * (scaled - unit_rows * jnp.mean(scaled * unit_rows, axis=-1, keepdims=True))
    return (result, jnp.sum(upstream * unit_rows, axis=0))


def rope_tables(position, half_dim):
    freq_table = ROPE_BASE ** (-(jnp.arange(half_dim, dtype=F32) * 2.0 / (2 * half_dim)))
    angle_table = position.astype(F32)[:, None] * freq_table[None, :]
    return (jnp.cos(angle_table), jnp.sin(angle_table))


def rope_turn(values, cosine, sine_table):
    half_dim = values.shape[-1] // 2
    lead_half = values[..., :half_dim]
    tail_half = values[..., half_dim:]
    return jnp.concatenate(
        [lead_half * cosine - tail_half * sine_table, tail_half * cosine + lead_half * sine_table],
        axis=-1,
    )


def rope_back(grad_rows, cosine, sine_table):
    return rope_turn(grad_rows, cosine, -sine_table)


def gated_unit(gate_in, up_in):
    return jax.nn.gelu(gate_in, approximate=True) * up_in


def adam_step(weight, first_old, second_old, gradient, step_rate, decay_rate):
    first_new = BETA_ONE * first_old + (1.0 - BETA_ONE) * gradient
    second_new = BETA_TWO * second_old + (1.0 - BETA_TWO) * gradient * gradient
    first_hat = first_new / (1.0 - BETA_ONE**STEP)
    second_hat = second_new / (1.0 - BETA_TWO**STEP)
    weight_new = weight - step_rate * (
        first_hat / (jnp.sqrt(second_hat) + EPS_ADAM) + decay_rate * weight
    )
    return (first_new, second_new, weight_new)


def block_weights(queries, keys, query_pos, key_pos):
    scores = jnp.einsum("kqd,krd->kqr", queries, keys, preferred_element_type=F32)
    unit = jnp.tanh(scores / SOFT_CAP)
    allowed = key_pos[None, None, :] <= query_pos[None, :, None]
    return (unit, jnp.where(allowed, jnp.exp(SOFT_CAP * unit), 0.0))


def block_forward(queries, keys, values, query_pos, key_pos):
    unused, weights = block_weights(queries, keys, query_pos, key_pos)
    return (
        jnp.sum(weights, axis=-1, keepdims=True),
        jnp.einsum("kqr,krd->kqd", weights.astype(BF16), values, preferred_element_type=F32),
    )


def block_backward(queries, keys, values, query_pos, key_pos, grad_summed, delta):
    unit, weights = block_weights(queries, keys, query_pos, key_pos)
    grad_weights = jnp.einsum("kqd,krd->kqr", grad_summed, values, preferred_element_type=F32)
    grad_scores = (weights * (grad_weights - delta) * (1.0 - unit * unit)).astype(BF16)
    return (
        jnp.einsum("kqr,krd->kqd", grad_scores, keys, preferred_element_type=F32),
        jnp.einsum("kqr,kqd->krd", grad_scores, queries, preferred_element_type=F32),
        jnp.einsum("kqr,kqd->krd", weights.astype(BF16), grad_summed, preferred_element_type=F32),
    )


def shards(
    tokens,
    positions,
    cotangent,
    qkv_weight,
    qkv_first,
    qkv_second,
    out_weight,
    out_first,
    out_second,
    gate_up,
    gate_up_first,
    gate_up_second,
    down_weight,
    down_first,
    down_second,
    gains,
    gains_first,
    gains_second,
):
    size_x, size_z, size_h = lax.axis_size("fsdp"), lax.axis_size("ctx"), lax.axis_size("head")
    z, own_h = lax.axis_index("ctx"), lax.axis_index("head")
    tok_rows, width = tokens.shape
    block_rows = tok_rows * size_h
    order = head_order()
    copies = max(1, size_h // KVH)
    kv_local = KVH * copies // size_h
    query_local = QH // size_h
    group = query_local // kv_local
    query_scale = 1.0 / math.sqrt(HD)
    query_cols, kv_cols = query_local * HD, kv_local * HD

    def positions_of(block):
        rows = lax.dynamic_slice_in_dim(positions, block * block_rows, block_rows)
        return jnp.concatenate(
            [lax.dynamic_slice_in_dim(rows, (own_h ^ one) * tok_rows, tok_rows) for one in order]
        )

    lines = Lines()

    pieces = head_exchange(lines, split_heads(qkv_weight, own_h))
    qkv_piece = join_rows(pieces, own_h)
    qkv_rows, local_cols = qkv_weight.shape[0], qkv_piece.shape[1]
    more_tokens = [tokens] + swap_top(lines, tokens) if size_h > 1 else [tokens]
    qkv_parts = spread_ctx(lines, qkv_piece, swap_fsdp)
    qkv_full = put_pieces(qkv_parts).reshape(width, local_cols)
    gain_rows = gather_gains(after(gains, qkv_piece))

    out_rows = out_weight.shape[0]
    out_groups = size_x * size_z // size_h
    out_low = after(out_weight, qkv_piece).astype(BF16)
    out_parts = spread_ctx(lines, out_low, swap_fsdp)
    out_own = put_pieces(out_parts).reshape(size_h, out_groups, out_rows, width)
    out_sets = head_exchange(lines, pick_pieces(out_own, [own_h ^ i for i in range(size_h)]))
    out_full = place(out_sets, [own_h ^ i for i in range(size_h)])
    out_full = jnp.transpose(out_full, (1, 0, 2, 3)).reshape(query_cols, width)

    ff_rows = gate_up.shape[1]
    ff_cols = gate_up.shape[2] // 2
    low = lax.rem(z, 2)
    down_turned = down_weight.T[None]
    gate_up_halves = split_units(after(gate_up, qkv_piece), low, 2)
    down_halves = split_units(after(down_turned, qkv_piece), low, 2)
    hops = range(2, size_z, 2)

    def far_units(one, k):
        return [(swap_ctx(lines, one, other), k ^ other) for other in hops]

    def unit_parts(pieces):
        return [unit_part(lines, one, k) for one, k in pieces]

    gate_up_parts = unit_parts([(gate_up_halves[0], 0)])
    gate_up_far = far_units(gate_up_halves[0], 0)
    gate_up_near = swap_ctx(lines, gate_up_halves[1], 1)
    down_near = swap_ctx(lines, down_halves[1], 1)
    gate_up_parts += unit_parts(gate_up_far) + unit_parts([(gate_up_near, 1)])

    block_tokens = head_gather(lines, jnp.concatenate(more_tokens), head_bits()[1:]).astype(F32)
    inputs = tokens.astype(F32)
    first_normed = rms_norm(block_tokens, gain_rows[0]).astype(BF16)
    projected = matmul(first_normed, qkv_full)
    block_pos = positions_of(z)
    cosine, sine_table = rope_tables(block_pos, HD // 2)

    def heads_of(values, count):
        return jnp.transpose(values.reshape(block_rows, count, HD), (1, 0, 2))

    queries = heads_of(projected[:, :query_cols], query_local)
    queries = (rope_turn(queries, cosine, sine_table) * query_scale).astype(BF16)
    queries = queries.reshape(kv_local, group * block_rows, HD)
    own_keys = heads_of(projected[:, query_cols : query_cols + kv_cols], kv_local)
    own_keys = rope_turn(own_keys, cosine, sine_table).astype(BF16)
    own_values = heads_of(projected[:, query_cols + kv_cols :], kv_local).astype(BF16)
    query_pos = jnp.tile(block_pos, group)
    own_kv = jnp.stack([own_keys, own_values])
    kv_slots = ctx_slots(lines, own_kv)
    down_parts = unit_parts([(down_halves[0], 0), (down_near, 1)])
    gate_up_parts += unit_parts(far_units(gate_up_near, 1))
    down_parts += unit_parts(far_units(down_halves[0], 0) + far_units(down_near, 1))
    pos_slots = [positions_of(lax.rem(z + k, size_z)) for k in range(size_z)]
    exp_total = 0.0
    summed = 0.0
    for kv_slot, key_pos in zip(kv_slots, pos_slots):
        total_part, summed_part = block_forward(
            queries, kv_slot[0], kv_slot[1], query_pos, key_pos
        )
        exp_total = exp_total + total_part
        summed = summed + summed_part
    attended = summed / exp_total

    def rows_of(heads):
        heads = heads.reshape(-1, block_rows, HD)
        return jnp.transpose(heads, (1, 0, 2)).reshape(block_rows, -1)

    attended_low = rows_of(attended.astype(BF16))
    attn_out = head_reduce(lines, matmul(attended_low, out_full).astype(BF16))
    middle = inputs + rms_norm(attn_out, gain_rows[1])
    second_normed = rms_norm(middle, gain_rows[2]).astype(BF16)

    low_bits, top_bits = head_bits()[1:], head_bits()[:1]

    def both_blocks(rows):
        other = swap_ctx(lines, rows, 1)
        return [head_gather(lines, rows), head_gather(lines, other)]

    def sum_blocks(parts):
        own, other = parts
        other = swap_ctx(lines, head_reduce(lines, other).astype(BF16), 1)
        return head_reduce(lines, own) + other.astype(F32)

    normed_slots = both_blocks(second_normed)
    gate_up_full = put_pieces(gate_up_parts).reshape(width, 2 * ff_cols)
    down_full = put_pieces(down_parts).reshape(width, ff_cols)
    act_slots = [matmul(rows, gate_up_full) for rows in normed_slots]
    hidden_slots = [
        gated_unit(act[:, :ff_cols], act[:, ff_cols:]).astype(BF16) for act in act_slots
    ]
    ffn_out = sum_blocks([matmul_nt(hidden, down_full).astype(BF16) for hidden in hidden_slots])
    mixed_out = (middle + rms_norm(ffn_out, gain_rows[3])).astype(BF16)

    upstream = cotangent.astype(F32)
    grad_ffn, gain_grad_ffn = norm_back(ffn_out, gain_rows[3], upstream)
    grad_slots = both_blocks(grad_ffn.astype(BF16))
    grad_act_slots, grad_second_parts = [], []
    for rows, act in zip(grad_slots, act_slots):
        grad_hidden = matmul(rows, down_full)
        unit_out, unit_back = jax.vjp(gated_unit, act[:, :ff_cols], act[:, ff_cols:])
        grad_act_slots.append(jnp.concatenate(unit_back(grad_hidden), axis=1).astype(BF16))
        grad_second_parts.append(matmul_nt(grad_act_slots[-1], gate_up_full).astype(BF16))
    other = head_reduce(lines, grad_second_parts[1]).astype(BF16)
    other_came = lines.head.came[-1] if size_h > 1 else ()
    other = swap_ctx(lines, other, 1)
    own = head_reduce(lines, grad_second_parts[0])
    down_rows = after(jnp.concatenate(grad_slots), grad_second_parts[1])
    down_term = matmul_tn(down_rows, jnp.concatenate(hidden_slots)).astype(BF16)
    down_back = units_back(lines, down_term.reshape(size_x * size_z, ff_rows, ff_cols))
    gate_up_rows = after(jnp.concatenate(normed_slots), down_term, *other_came)
    gate_up_term = matmul_tn(gate_up_rows, jnp.concatenate(grad_act_slots))
    gate_up_term = gate_up_term.astype(BF16)
    grad_second = own + other.astype(F32)
    down_other = units_sent(lines, down_back, 1, other)
    down_back = [units_sent(lines, down_back, 0), down_other]
    gate_up_back = units_back(lines, gate_up_term.reshape(size_x * size_z, ff_rows, 2 * ff_cols))
    gate_up_other = units_sent(lines, gate_up_back, 1)

    grad_middle_part, gain_grad_middle = norm_back(middle, gain_rows[2], grad_second)
    grad_middle = upstream + grad_middle_part
    grad_attn, gain_grad_attn = norm_back(attn_out, gain_rows[1], grad_middle)
    block_grad_attn = head_gather(lines, grad_attn.astype(BF16))
    out_term = matmul_tn(attended_low, block_grad_attn).astype(BF16)
    out_term = jnp.transpose(
        out_term.reshape(out_groups, size_h, out_rows, width), (1, 0, 2, 3)
    )
    grad_attended = matmul_nt(block_grad_attn, out_full).astype(BF16)
    grad_attended = heads_of(grad_attended, query_local).astype(F32)
    grad_attended = grad_attended.reshape(kv_local, group * block_rows, HD)
    row_delta = jnp.sum(grad_attended * attended, axis=-1, keepdims=True)
    delta = row_delta / exp_total
    grad_summed = (grad_attended / exp_total).astype(BF16)
    grad_query = 0.0
    kv_parts = {}
    for k in ctx_order():
        query_part, key_part, value_part = block_backward(
            queries, kv_slots[k][0], kv_slots[k][1], query_pos, pos_slots[k], grad_summed, delta
        )
        grad_query = grad_query + query_part
        kv_parts[k] = jnp.stack([key_part, value_part])
    grad_kv = sum_ctx_slots(lines, lambda k: kv_parts[k])
    gate_up_back = [units_sent(lines, gate_up_back, 0), gate_up_other]
    out_sets = head_exchange(lines, pick_pieces(out_term, [own_h ^ i for i in range(size_h)]))
    out_term = place(out_sets, [own_h ^ i for i in range(size_h)])

    grad_query = grad_query.astype(BF16).astype(F32).reshape(query_local, block_rows, HD)
    query_proj = rows_of(rope_back(grad_query, cosine, sine_table) * query_scale).astype(BF16)
    grad_kv = grad_kv.astype(BF16).astype(F32)
    kv_proj = jnp.concatenate(
        [rows_of(rope_back(grad_kv[0], cosine, sine_table)), rows_of(grad_kv[1])], axis=1
    ).astype(BF16)
    grad_proj = jnp.concatenate([query_proj, kv_proj], axis=1)
    qkv_term = matmul_tn(first_normed, grad_proj).astype(BF16)
    qkv_sums = sum_over_fsdp(
        lines, qkv_term.reshape(size_x * size_z, size_h * qkv_rows, local_cols), ctx_order()
    )
    qkv_sum = sum_ctx_slots(lines, lambda k: qkv_sums[k])
    grad_first = head_reduce(lines, matmul_nt(grad_proj, qkv_full).astype(BF16))
    grad_input_part, gain_grad_input = norm_back(inputs, gain_rows[0], grad_first)
    tokens_grad = (grad_middle + grad_input_part).astype(BF16)

    qkv_pieces = head_exchange(lines, split_rows([qkv_sum], own_h))
    out_sums = sum_over_fsdp(
        lines, out_term.reshape(size_x * size_z, out_rows, width), ctx_order()
    )
    out_grad = sum_ctx_slots(lines, lambda k: out_sums[k])
    gains_grad = scatter_gains(
        jnp.stack([gain_grad_input, gain_grad_attn, gain_grad_middle, gain_grad_ffn])
    )

    qkv_grad, qkv_first_new, qkv_second_new, qkv_new = adam_qkv(
        [one[:, :query_cols] for one in qkv_pieces],
        [one[:, query_cols:] for one in qkv_pieces],
        own_h, qkv_weight, qkv_first, qkv_second
    )
    out_first_new, out_second_new, out_new = adam_step(
        out_weight, out_first, out_second, out_grad, RATE_MATRIX, WEIGHT_DECAY
    )
    gate_up_grad, gate_up_first_new, gate_up_second_new, gate_up_new = adam_units(
        gate_up_back, low, gate_up, gate_up_first, gate_up_second, RATE_MATRIX
    )
    down_outs = adam_units(
        down_back,
        low,
        down_turned,
        down_first.T[None],
        down_second.T[None],
        RATE_DOWN,
    )
    down_grad, down_first_new, down_second_new, down_new = [one[0].T for one in down_outs]
    gains_first_new, gains_second_new, gains_new = adam_step(
        gains, gains_first, gains_second, gains_grad, RATE_GAIN, 0.0
    )
    return (
        mixed_out,
        tokens_grad,
        qkv_grad,
        qkv_first_new,
        qkv_second_new,
        qkv_new,
        out_grad,
        out_first_new,
        out_second_new,
        out_new,
        gate_up_grad,
        gate_up_first_new,
        gate_up_second_new,
        gate_up_new,
        down_grad,
        down_first_new,
        down_second_new,
        down_new,
        gains_grad,
        gains_first_new,
        gains_second_new,
        gains_new,
    )


TOKEN_SPEC = P(("fsdp", "ctx", "head"), None)
GATE_UP_SPEC = P(None, ("fsdp", "ctx"), "head")
DOWN_SPEC = P("head", ("fsdp", "ctx"))


def solution(mesh):
    in_specs = (
        (TOKEN_SPEC, P("fsdp"))
        + (TOKEN_SPEC,) * 7
        + (GATE_UP_SPEC,) * 3
        + (DOWN_SPEC,) * 3
        + (TOKEN_SPEC,) * 3
    )
    out_specs = (
        (TOKEN_SPEC,) * 10 + (GATE_UP_SPEC,) * 4 + (DOWN_SPEC,) * 4 + (TOKEN_SPEC,) * 4
    )
    return jax.shard_map(shards, mesh=mesh, in_specs=in_specs, out_specs=out_specs, check_vma=False)
```

```python
import functools
import math

import jax
import jax.numpy as jnp
from jax import lax
from jax.experimental import pallas as pl
from jax.experimental.pallas import tpu as pltpu
from jax.sharding import PartitionSpec as P

QH = 8
KVH = 4
HD = 256
STEP = 10


SOFT_CAP = 50.0
EPS_NORM = 1e-06
ROPE_BASE = 10000.0
BETA_ONE = 0.9
BETA_TWO = 0.95
EPS_ADAM = 1e-08
RATE_MATRIX = 0.05
RATE_DOWN = 0.025
RATE_GAIN = 0.5
WEIGHT_DECAY = 0.1

BF16 = jnp.bfloat16
F32 = jnp.float32


def after(values, *others):
    return lax.optimization_barrier((values,) + others)[0]


class Line:
    def __init__(self, depth):
        self.depth = depth
        self.came = []

    def send(self, sendings):
        values = tuple(one for one, _, _ in sendings)
        if len(self.came) >= self.depth:
            values = after(values, *self.came[-self.depth])
        results = [
            lax.ppermute(one, axes, pairs) for one, (_, axes, pairs) in zip(values, sendings)
        ]
        self.came.append(tuple(results))
        return results


class Lines:
    def __init__(self):
        self.fsdp, self.ctx, self.head, self.pair = Line(2), Line(2), Line(2), Line(2)


DEPTH = 2


def ring_pairs(size, step):
    return [(i, (i + step) % size) for i in range(size)]


def swap_bit(lines, values, bit):
    size = lax.axis_size("head")
    pairs = [(i, i ^ bit) for i in range(size)]
    if bit == 1 and size > 2:
        return lax.ppermute(values, "head", pairs)
    return lines.head.send([(values, "head", pairs)])[0]


def send_ctx(lines, values, step):
    return lines.ctx.send([(values, "ctx", ring_pairs(lax.axis_size("ctx"), step))])[0]


def swap_ctx(lines, values, other):
    pairs = [(z, z ^ other) for z in range(lax.axis_size("ctx"))]
    line = lines.pair if other == 1 else lines.ctx
    return line.send([(values, "ctx", pairs)])[0]


def unit_part(lines, one, other):
    return ([one] + swap_fsdp(lines, one), lambda z: z ^ other, lambda z: z >= 0)


def units_back(lines, pieces):
    size_x, size_z = lax.axis_size("fsdp"), lax.axis_size("ctx")
    x, z = lax.axis_index("fsdp"), lax.axis_index("ctx")
    order = [k ^ 1 for k in range(2, size_z)] + [1, 0]
    chosen = [(k, step) for k in order for step in range(size_x)]
    picked = pick_pieces(
        pieces, [lax.rem(x + step, size_x) * size_z + (z ^ k) for k, step in chosen]
    )
    picked = dict(zip(chosen, picked))
    sums = {}
    for k in order:
        sums[k] = picked[k, 0].astype(F32)
        for step in range(1, size_x):
            pairs = ring_pairs(size_x, step)
            came = lines.fsdp.send([(picked[k, step], "fsdp", pairs)])[0]
            sums[k] = sums[k] + came.astype(F32)
    return sums


def units_sent(lines, sums, low, *others):
    total = sums[low]
    for other in range(2, lax.axis_size("ctx"), 2):
        one = sums[other ^ low].astype(BF16)
        one = swap_ctx(lines, after(one, *others) if others else one, other)
        total = total + one.astype(F32)
    return swap_ctx(lines, total.astype(BF16), 1) if low else total


def swap_fsdp(lines, values, valid=lambda z: True):
    size_x, size_z = lax.axis_size("fsdp"), lax.axis_size("ctx")
    return [
        lines.fsdp.send(
            [
                (
                    values,
                    ("fsdp", "ctx"),
                    [
                        (x * size_z + z, (x + step) % size_x * size_z + z)
                        for x in range(size_x)
                        for z in range(size_z)
                        if valid(z)
                    ],
                )
            ]
        )[0]
        for step in range(1, size_x)
    ]


def swap_top(lines, values, valid=lambda z: True):
    size_z, size_h = lax.axis_size("ctx"), lax.axis_size("head")
    pairs = [
        (z * size_h + h, z * size_h + (h ^ (size_h // 2)))
        for z in range(size_z)
        for h in range(size_h)
        if valid(z)
    ]
    return lines.head.send([(values, ("ctx", "head"), pairs)])


def head_bits():
    bits = []
    bit = lax.axis_size("head") // 2
    while bit:
        bits.append(bit)
        bit //= 2
    return bits


def head_order():
    order = [0]
    for bit in head_bits():
        order = order + [one ^ bit for one in order]
    return order


def head_gather(lines, rows, bits=None):
    for bit in head_bits() if bits is None else bits:
        rows = jnp.concatenate([rows, swap_bit(lines, rows, bit)], axis=0)
    return rows


def head_reduce(lines, part):
    for bit in reversed(head_bits()):
        half = part.shape[0] // 2
        came = swap_bit(lines, part[half:].astype(BF16), bit)
        part = part[:half].astype(F32) + came.astype(F32)
    return part


def head_exchange(lines, pieces):
    return [pieces[0]] + [swap_bit(lines, pieces[i], i) for i in range(1, len(pieces))]


AHEAD, BACK = [(0, 1), (1, 2), (2, 3)], [(1, 0), (2, 1), (3, 2)]
TWO, ENDS = [(0, 2), (1, 3), (2, 0), (3, 1)], [(2, 3), (1, 0)]
FAR = [(0, 1), (3, 2)]


def spread_ctx(lines, own, swaps):
    size = lax.axis_size("ctx")
    always = lambda z: z >= 0
    parts = [([own] + swaps(lines, own), lambda z: z, always)]
    if size != 4:
        for k in range(1, size):
            one = send_ctx(lines, own, k)
            source = lambda z, k=k: (z - k + size) % size
            parts.append(([one] + swaps(lines, one), source, always))
        return parts
    not_first, not_last, at_end = lambda z: z >= 1, lambda z: z <= 2, lambda z: z % 3 == 0
    ahead, back = lines.ctx.send([(own, "ctx", AHEAD), (own, "ctx", BACK)])
    two = lines.ctx.send([(after(own, ahead, back), "ctx", TWO)])[0]
    parts.append(([ahead] + swaps(lines, ahead, not_first), lambda z: z - 1, not_first))
    parts.append(([back] + swaps(lines, back, not_last), lambda z: z + 1, not_last))
    two = after(two, *parts[1][0][1:])
    ends = lines.ctx.send([(two, "ctx", ENDS)])[0]
    parts.append(([two] + swaps(lines, two), lambda z: z ^ 2, always))
    parts.append(([ends] + swaps(lines, ends, at_end), lambda z: 3 - z, at_end))
    return parts


def put_pieces(parts):
    size_x, size_z = lax.axis_size("fsdp"), lax.axis_size("ctx")
    x, z = lax.axis_index("fsdp"), lax.axis_index("ctx")
    arrays, places = [], []
    for by_step, source, valid in parts:
        for step, one in enumerate(by_step):
            at = lax.rem(x - step + size_x, size_x) * size_z + source(z)
            arrays.append(one)
            places.append(jnp.where(valid(z), at, -1))
    return place(arrays, places, size_x * size_z)


def ctx_slots(lines, values, swaps=lambda lines, values, valid=None: [], join=lambda arrays: arrays[0]):
    size = lax.axis_size("ctx")
    arrays = [join(by_step) for by_step, _, _ in spread_ctx(lines, values, swaps)]
    if size != 4:
        return [arrays[0]] + [arrays[size - k] for k in range(1, size)]
    z = lax.axis_index("ctx")
    own, ahead, back, two, ends = arrays
    return [own, jnp.where(z == 3, ends, back), two, jnp.where(z == 0, ends, ahead)]


def sum_ctx_slots(lines, part_of):
    size = lax.axis_size("ctx")
    z = lax.axis_index("ctx")
    if size != 4:
        total = 0.0
        for k in ctx_order():
            part = part_of(k)
            total = total + (send_ctx(lines, part.astype(BF16), k).astype(F32) if k else part)
        return total
    part_one = part_of(1).astype(BF16)
    part_three = part_of(3).astype(BF16)
    far = lines.ctx.send([(jnp.where(z == 0, part_three, part_one), "ctx", FAR)])[0]
    ahead, back = lines.ctx.send([(part_one, "ctx", AHEAD), (part_three, "ctx", BACK)])
    part_two = part_of(2).astype(F32) + far.astype(F32)
    two = lines.ctx.send([(part_two.astype(BF16), "ctx", TWO)])[0]
    return part_of(0).astype(F32) + ahead.astype(F32) + back.astype(F32) + two.astype(F32)


def far_first(size):
    return sorted(range(size), key=lambda k: -min(k, size - k))


def ctx_order():
    size = lax.axis_size("ctx")
    return [1, 3, 2, 0] if size == 4 else far_first(size)


def sum_over_fsdp(lines, pieces, order):
    size_x, size_z = lax.axis_size("fsdp"), lax.axis_size("ctx")
    x, z = lax.axis_index("fsdp"), lax.axis_index("ctx")
    chosen = [(k, step) for k in order for step in range(size_x)]
    picked = pick_pieces(
        pieces,
        [lax.rem(x + step, size_x) * size_z + lax.rem(z + k, size_z) for k, step in chosen],
    )
    picked = dict(zip(chosen, picked))
    sums = {}
    for k in order:
        total = picked[k, 0].astype(F32)
        for step in range(1, size_x):
            pairs = ring_pairs(size_x, step)
            total = total + lines.fsdp.send([(picked[k, step], "fsdp", pairs)])[0].astype(F32)
        sums[k] = total
    return sums


def exchange_all(pieces):
    return lax.all_to_all(
        pieces, ("fsdp", "ctx", "head"), split_axis=0, concat_axis=0, tiled=True
    )


def device_count():
    return lax.axis_size("fsdp") * lax.axis_size("ctx") * lax.axis_size("head")


def gather_gains(gains):
    rows = exchange_all(jnp.broadcast_to(gains.astype(BF16).T[None], (device_count(),) + gains.shape[::-1]))
    return jnp.transpose(rows, (1, 0, 2)).reshape(gains.shape[1], -1).astype(F32)


def scatter_gains(rows):
    pieces = jnp.transpose(rows.reshape(rows.shape[0], device_count(), -1), (1, 0, 2))
    return jnp.sum(exchange_all(pieces), axis=0).T


ANYWHERE = pl.BlockSpec(memory_space=pl.ANY)
SCALARS = pl.BlockSpec(memory_space=pltpu.SMEM)
IN_VMEM = pl.BlockSpec(memory_space=pltpu.VMEM)
VMEM_LIMIT = 48 * 1024 * 1024


def scalars(*values):
    return jnp.stack([jnp.asarray(one, jnp.int32) for one in values])


def cost(byte_count, flops=0):
    return pl.CostEstimate(flops=flops, bytes_accessed=byte_count, transcendentals=0)


def params():
    return pltpu.CompilerParams(vmem_limit_bytes=VMEM_LIMIT)


def place(pieces, places, total=None):
    count = len(pieces)
    shape = (total or count,) + pieces[0].shape

    def kernel(places_ref, *refs):
        out_ref, sems = refs[count], refs[count + 1]

        def each(act):
            for i in range(count):
                copy = pltpu.make_async_copy(
                    refs[i], out_ref.at[jnp.maximum(places_ref[i], 0)], sems.at[i]
                )
                pl.when(places_ref[i] >= 0)(functools.partial(act, copy))

        each(lambda copy: copy.start())
        each(lambda copy: copy.wait())

    return pl.pallas_call(
        kernel,
        out_shape=jax.ShapeDtypeStruct(shape, pieces[0].dtype),
        in_specs=[SCALARS] + [ANYWHERE] * count,
        out_specs=IN_VMEM,
        scratch_shapes=[pltpu.SemaphoreType.DMA((count,))],
        compiler_params=params(),
        cost_estimate=cost(2 * math.prod(shape) * pieces[0].dtype.itemsize),
        name="place",
    )(scalars(*places), *pieces)


def pick_pieces(stacked, places):
    count = len(places)
    shape = stacked.shape[1:]

    def kernel(places_ref, in_ref, *refs):
        sems = refs[count]
        copies = [
            pltpu.make_async_copy(in_ref.at[places_ref[i]], refs[i], sems.at[i])
            for i in range(count)
        ]
        for copy in copies:
            copy.start()
        for copy in copies:
            copy.wait()

    return pl.pallas_call(
        kernel,
        out_shape=[jax.ShapeDtypeStruct(shape, stacked.dtype)] * count,
        in_specs=[SCALARS, IN_VMEM],
        out_specs=[ANYWHERE] * count,
        scratch_shapes=[pltpu.SemaphoreType.DMA((count,))],
        compiler_params=params(),
        cost_estimate=cost(2 * count * math.prod(shape) * stacked.dtype.itemsize),
        name="pick_pieces",
    )(scalars(*places), stacked)


def kv_start(head):
    return lax.div(head * KVH, lax.axis_size("head")) * HD


def split_heads(weight, own):
    rows = weight.shape[0]
    size = lax.axis_size("head")
    query_cols, kv_cols = QH * HD // size, max(1, KVH // size) * HD
    local_cols = query_cols + 2 * kv_cols

    def kernel(own_ref, weight_ref, *outs):
        for other in range(size):
            head = own_ref[0] ^ other
            starts = (head * query_cols, QH * HD + kv_start(head), (QH + KVH) * HD + kv_start(head))
            at = 0
            for start, count in zip(starts, (query_cols, kv_cols, kv_cols)):
                columns = pl.ds(pl.multiple_of(start, HD), count)
                outs[other][:, at : at + count] = weight_ref[:, columns].astype(BF16)
                at += count

    return pl.pallas_call(
        kernel,
        out_shape=[jax.ShapeDtypeStruct((rows, local_cols), BF16)] * size,
        in_specs=[SCALARS, IN_VMEM],
        out_specs=[IN_VMEM] * size,
        compiler_params=params(),
        cost_estimate=cost(weight.size * 6),
        name="split_heads",
    )(scalars(own), weight)


def join_rows(pieces, own):
    rows, cols = pieces[0].shape
    size = len(pieces)
    if rows % 8:
        stacked = jnp.stack(pieces)
        return stacked[own ^ jnp.arange(size)].reshape(size * rows, cols)

    def kernel(own_ref, *refs):
        out_ref, wide_ref = refs[size], refs[size + 1]
        for other in range(size):
            at = pl.multiple_of((own_ref[0] ^ other) * rows, 8)
            wide_ref[pl.ds(at, rows), :] = refs[other][...].astype(F32)
        out_ref[...] = wide_ref[...].astype(BF16)

    return pl.pallas_call(
        kernel,
        out_shape=jax.ShapeDtypeStruct((size * rows, cols), BF16),
        in_specs=[SCALARS] + [IN_VMEM] * size,
        out_specs=IN_VMEM,
        scratch_shapes=[pltpu.VMEM((size * rows, cols), F32)],
        compiler_params=params(),
        cost_estimate=cost(size * rows * cols * 4),
        name="join_rows",
    )(scalars(own), *pieces)


def split_rows(parts, own):
    size = lax.axis_size("head")
    rows, cols = parts[0].shape[0] // size, parts[0].shape[1]
    if rows % 8:
        total = sum(part.astype(F32) for part in parts).reshape(size, rows, cols)
        total = total[own ^ jnp.arange(size)].astype(BF16)
        return [total[other] for other in range(size)]

    def kernel(own_ref, *refs):
        outs, wide_ref = refs[len(parts) : -1], refs[-1]
        total = refs[0][...].astype(F32)
        for part in refs[1 : len(parts)]:
            total = total + part[...].astype(F32)
        wide_ref[...] = total
        for other in range(size):
            at = pl.multiple_of((own_ref[0] ^ other) * rows, 8)
            outs[other][...] = wide_ref[pl.ds(at, rows), :].astype(BF16)

    return pl.pallas_call(
        kernel,
        out_shape=[jax.ShapeDtypeStruct((rows, cols), BF16)] * size,
        in_specs=[SCALARS] + [IN_VMEM] * len(parts),
        out_specs=[IN_VMEM] * size,
        scratch_shapes=[pltpu.VMEM((size * rows, cols), F32)],
        compiler_params=params(),
        cost_estimate=cost(size * rows * cols * 12),
        name="split_rows",
    )(scalars(own), *parts)


def row_block(rows, most):
    return max(one for one in range(1, rows + 1) if rows % one == 0 and one <= most and (one % 16 == 0 or one == rows))


def split_units(weight, own, size):
    count, rows, cols = weight.shape[0], weight.shape[1], weight.shape[2] // size
    block = row_block(rows, 96)

    def kernel(own_ref, in_ref, *refs):
        outs, kept = refs[:size], refs[size]
        for part in range(size):
            for one in range(count):
                kept[part, :, one * cols : (one + 1) * cols] = in_ref[
                    one, :, part * cols : (part + 1) * cols
                ]
        for k in range(size):
            outs[k][...] = kept[own_ref[0] ^ k].astype(BF16)

    return pl.pallas_call(
        kernel,
        grid=(rows // block,),
        out_shape=[jax.ShapeDtypeStruct((rows, count * cols), BF16)] * size,
        in_specs=[SCALARS, pl.BlockSpec((count, block, size * cols), lambda i: (0, i, 0))],
        out_specs=[pl.BlockSpec((block, count * cols), lambda i: (i, 0))] * size,
        scratch_shapes=[pltpu.VMEM((size, block, count * cols), F32)],
        compiler_params=params(),
        cost_estimate=cost(weight.size * 6),
        name="split_units",
    )(scalars(own), weight)


def adam_units(came, own, weight, first_old, second_old, step_rate):
    size = len(came)
    count = weight.shape[0]
    rows, cols = came[0].shape[0], came[0].shape[1] // count
    block = row_block(rows, 96 // count)

    def kernel(own_ref, *refs):
        pieces, (weight_ref, first_ref, second_ref) = refs[:size], refs[size : size + 3]
        outs, kept = refs[size + 3 : size + 7], refs[size + 7]
        for k in range(size):
            kept[own_ref[0] ^ k] = pieces[k][...].astype(F32)
        for part in range(size):
            for one in range(count):
                outs[0][one, :, part * cols : (part + 1) * cols] = kept[
                    part, :, one * cols : (one + 1) * cols
                ]
        outs[1][...], outs[2][...], outs[3][...] = adam_step(
            weight_ref[...], first_ref[...], second_ref[...], outs[0][...], step_rate, WEIGHT_DECAY
        )

    whole = pl.BlockSpec((count, block, size * cols), lambda i: (0, i, 0))
    return pl.pallas_call(
        kernel,
        grid=(rows // block,),
        out_shape=[jax.ShapeDtypeStruct(weight.shape, F32)] * 4,
        in_specs=[SCALARS]
        + [pl.BlockSpec((block, count * cols), lambda i: (i, 0))] * size
        + [whole] * 3,
        out_specs=[whole] * 4,
        scratch_shapes=[pltpu.VMEM((size, block, count * cols), F32)],
        compiler_params=params(),
        cost_estimate=cost(weight.size * 30),
        name="adam_units",
    )(scalars(own), *came, weight, first_old, second_old)


def adam_qkv(query_pieces, kv_pieces, own, weight, first_old, second_old):
    size = len(query_pieces)
    query_cols, kv_cols = query_pieces[0].shape[1], kv_pieces[0].shape[1] // 2

    def kernel(own_ref, *refs):
        (weight_ref, first_ref, second_ref), outs = refs[2 * size : 2 * size + 3], refs[2 * size + 3 :]
        grad_ref = outs[0]
        if size > KVH:
            grad_ref[:, QH * HD :] = jnp.zeros_like(grad_ref[:, QH * HD :])
        for other in range(size):
            head = own_ref[0] ^ other
            columns = pl.ds(pl.multiple_of(head * query_cols, HD), query_cols)
            grad_ref[:, columns] = refs[other][...].astype(F32)
            for at in (0, 1):
                start = (QH + at * KVH) * HD + kv_start(head)
                columns = pl.ds(pl.multiple_of(start, HD), kv_cols)
                piece = refs[size + other][:, at * kv_cols : (at + 1) * kv_cols].astype(F32)
                if size > KVH:
                    piece = piece + grad_ref[:, columns]
                grad_ref[:, columns] = piece
        outs[1][...], outs[2][...], outs[3][...] = adam_step(
            weight_ref[...], first_ref[...], second_ref[...], grad_ref[...], RATE_MATRIX, WEIGHT_DECAY
        )

    return pl.pallas_call(
        kernel,
        out_shape=[jax.ShapeDtypeStruct(weight.shape, F32)] * 4,
        in_specs=[SCALARS] + [IN_VMEM] * (2 * size + 3),
        out_specs=[IN_VMEM] * 4,
        compiler_params=params(),
        cost_estimate=cost(weight.size * 30),
        name="adam_qkv",
    )(scalars(own), *query_pieces, *kv_pieces, weight, first_old, second_old)


def matmul(left, right):
    return jnp.dot(left, right, preferred_element_type=F32)


def matmul_nt(left, right):
    return lax.dot_general(left, right, (((1,), (1,)), ((), ())), preferred_element_type=F32)


def matmul_tn(left, right):
    return lax.dot_general(left, right, (((0,), (0,)), ((), ())), preferred_element_type=F32)


def rms_norm(values, gain_row):
    inv_scale = lax.rsqrt(jnp.mean(values * values, axis=-1, keepdims=True) + EPS_NORM)
    return values * inv_scale * (1.0 + gain_row)


def norm_back(values, gain_row, upstream):
    inv_scale = lax.rsqrt(jnp.mean(values * values, axis=-1, keepdims=True) + EPS_NORM)
    unit_rows = values * inv_scale
    scaled = upstream * (1.0 + gain_row)
    result = inv_scale * (scaled - unit_rows * jnp.mean(scaled * unit_rows, axis=-1, keepdims=True))
    return (result, jnp.sum(upstream * unit_rows, axis=0))


def rope_tables(position, half_dim):
    freq_table = ROPE_BASE ** (-(jnp.arange(half_dim, dtype=F32) * 2.0 / (2 * half_dim)))
    angle_table = position.astype(F32)[:, None] * freq_table[None, :]
    return (jnp.cos(angle_table), jnp.sin(angle_table))


def rope_turn(values, cosine, sine_table):
    half_dim = values.shape[-1] // 2
    lead_half = values[..., :half_dim]
    tail_half = values[..., half_dim:]
    return jnp.concatenate(
        [lead_half * cosine - tail_half * sine_table, tail_half * cosine + lead_half * sine_table],
        axis=-1,
    )


def rope_back(grad_rows, cosine, sine_table):
    return rope_turn(grad_rows, cosine, -sine_table)


def gated_unit(gate_in, up_in):
    return jax.nn.gelu(gate_in, approximate=True) * up_in


def adam_step(weight, first_old, second_old, gradient, step_rate, decay_rate):
    first_new = BETA_ONE * first_old + (1.0 - BETA_ONE) * gradient
    second_new = BETA_TWO * second_old + (1.0 - BETA_TWO) * gradient * gradient
    first_hat = first_new / (1.0 - BETA_ONE**STEP)
    second_hat = second_new / (1.0 - BETA_TWO**STEP)
    weight_new = weight - step_rate * (
        first_hat / (jnp.sqrt(second_hat) + EPS_ADAM) + decay_rate * weight
    )
    return (first_new, second_new, weight_new)


def block_weights(queries, keys, query_pos, key_pos):
    scores = jnp.einsum("kqd,krd->kqr", queries, keys, preferred_element_type=F32)
    unit = jnp.tanh(scores / SOFT_CAP)
    allowed = key_pos[None, None, :] <= query_pos[None, :, None]
    return (unit, jnp.where(allowed, jnp.exp(SOFT_CAP * unit), 0.0))


def block_forward(queries, keys, values, query_pos, key_pos):
    unused, weights = block_weights(queries, keys, query_pos, key_pos)
    return (
        jnp.sum(weights, axis=-1, keepdims=True),
        jnp.einsum("kqr,krd->kqd", weights.astype(BF16), values, preferred_element_type=F32),
    )


def block_backward(queries, keys, values, query_pos, key_pos, grad_summed, delta):
    unit, weights = block_weights(queries, keys, query_pos, key_pos)
    grad_weights = jnp.einsum("kqd,krd->kqr", grad_summed, values, preferred_element_type=F32)
    grad_scores = (weights * (grad_weights - delta) * (1.0 - unit * unit)).astype(BF16)
    return (
        jnp.einsum("kqr,krd->kqd", grad_scores, keys, preferred_element_type=F32),
        jnp.einsum("kqr,kqd->krd", grad_scores, queries, preferred_element_type=F32),
        jnp.einsum("kqr,kqd->krd", weights.astype(BF16), grad_summed, preferred_element_type=F32),
    )


def shards(
    tokens,
    positions,
    cotangent,
    qkv_weight,
    qkv_first,
    qkv_second,
    out_weight,
    out_first,
    out_second,
    gate_up,
    gate_up_first,
    gate_up_second,
    down_weight,
    down_first,
    down_second,
    gains,
    gains_first,
    gains_second,
):
    size_x, size_z, size_h = lax.axis_size("fsdp"), lax.axis_size("ctx"), lax.axis_size("head")
    z, own_h = lax.axis_index("ctx"), lax.axis_index("head")
    tok_rows, width = tokens.shape
    block_rows = tok_rows * size_h
    order = head_order()
    copies = max(1, size_h // KVH)
    kv_local = KVH * copies // size_h
    query_local = QH // size_h
    group = query_local // kv_local
    query_scale = 1.0 / math.sqrt(HD)
    query_cols, kv_cols = query_local * HD, kv_local * HD

    def positions_of(block):
        rows = lax.dynamic_slice_in_dim(positions, block * block_rows, block_rows)
        return jnp.concatenate(
            [lax.dynamic_slice_in_dim(rows, (own_h ^ one) * tok_rows, tok_rows) for one in order]
        )

    lines = Lines()

    pieces = head_exchange(lines, split_heads(qkv_weight, own_h))
    qkv_piece = join_rows(pieces, own_h)
    qkv_rows, local_cols = qkv_weight.shape[0], qkv_piece.shape[1]
    more_tokens = [tokens] + swap_top(lines, tokens) if size_h > 1 else [tokens]
    qkv_parts = spread_ctx(lines, qkv_piece, swap_fsdp)
    qkv_full = put_pieces(qkv_parts).reshape(width, local_cols)
    gain_rows = gather_gains(after(gains, qkv_piece))

    out_rows = out_weight.shape[0]
    out_groups = size_x * size_z // size_h
    out_low = after(out_weight, qkv_piece).astype(BF16)
    out_parts = spread_ctx(lines, out_low, swap_fsdp)
    out_own = put_pieces(out_parts).reshape(size_h, out_groups, out_rows, width)
    out_sets = head_exchange(lines, pick_pieces(out_own, [own_h ^ i for i in range(size_h)]))
    out_full = place(out_sets, [own_h ^ i for i in range(size_h)])
    out_full = jnp.transpose(out_full, (1, 0, 2, 3)).reshape(query_cols, width)

    ff_rows = gate_up.shape[1]
    ff_cols = gate_up.shape[2] // 2
    low = lax.rem(z, 2)
    down_turned = down_weight.T[None]
    gate_up_halves = split_units(after(gate_up, qkv_piece), low, 2)
    down_halves = split_units(after(down_turned, qkv_piece), low, 2)
    hops = range(2, size_z, 2)

    def far_units(one, k):
        return [(swap_ctx(lines, one, other), k ^ other) for other in hops]

    def unit_parts(pieces):
        return [unit_part(lines, one, k) for one, k in pieces]

    gate_up_parts = unit_parts([(gate_up_halves[0], 0)])
    gate_up_far = far_units(gate_up_halves[0], 0)
    gate_up_near = swap_ctx(lines, gate_up_halves[1], 1)
    down_near = swap_ctx(lines, down_halves[1], 1)
    gate_up_parts += unit_parts(gate_up_far) + unit_parts([(gate_up_near, 1)])

    block_tokens = head_gather(lines, jnp.concatenate(more_tokens), head_bits()[1:]).astype(F32)
    inputs = tokens.astype(F32)
    first_normed = rms_norm(block_tokens, gain_rows[0]).astype(BF16)
    projected = matmul(first_normed, qkv_full)
    block_pos = positions_of(z)
    cosine, sine_table = rope_tables(block_pos, HD // 2)

    def heads_of(values, count):
        return jnp.transpose(values.reshape(block_rows, count, HD), (1, 0, 2))

    queries = heads_of(projected[:, :query_cols], query_local)
    queries = (rope_turn(queries, cosine, sine_table) * query_scale).astype(BF16)
    queries = queries.reshape(kv_local, group * block_rows, HD)
    own_keys = heads_of(projected[:, query_cols : query_cols + kv_cols], kv_local)
    own_keys = rope_turn(own_keys, cosine, sine_table).astype(BF16)
    own_values = heads_of(projected[:, query_cols + kv_cols :], kv_local).astype(BF16)
    query_pos = jnp.tile(block_pos, group)
    own_kv = jnp.stack([own_keys, own_values])
    kv_slots = ctx_slots(lines, own_kv)
    down_parts = unit_parts([(down_halves[0], 0), (down_near, 1)])
    gate_up_parts += unit_parts(far_units(gate_up_near, 1))
    down_parts += unit_parts(far_units(down_halves[0], 0) + far_units(down_near, 1))
    pos_slots = [positions_of(lax.rem(z + k, size_z)) for k in range(size_z)]
    exp_total = 0.0
    summed = 0.0
    for kv_slot, key_pos in zip(kv_slots, pos_slots):
        total_part, summed_part = block_forward(
            queries, kv_slot[0], kv_slot[1], query_pos, key_pos
        )
        exp_total = exp_total + total_part
        summed = summed + summed_part
    attended = summed / exp_total

    def rows_of(heads):
        heads = heads.reshape(-1, block_rows, HD)
        return jnp.transpose(heads, (1, 0, 2)).reshape(block_rows, -1)

    attended_low = rows_of(attended.astype(BF16))
    attn_out = head_reduce(lines, matmul(attended_low, out_full).astype(BF16))
    middle = inputs + rms_norm(attn_out, gain_rows[1])
    second_normed = rms_norm(middle, gain_rows[2]).astype(BF16)

    low_bits, top_bits = head_bits()[1:], head_bits()[:1]

    def both_blocks(rows):
        other = swap_ctx(lines, rows, 1)
        return [head_gather(lines, rows), head_gather(lines, other)]

    def sum_blocks(parts):
        own, other = parts
        other = swap_ctx(lines, head_reduce(lines, other).astype(BF16), 1)
        return head_reduce(lines, own) + other.astype(F32)

    normed_slots = both_blocks(second_normed)
    gate_up_full = put_pieces(gate_up_parts).reshape(width, 2 * ff_cols)
    down_full = put_pieces(down_parts).reshape(width, ff_cols)
    act_slots = [matmul(rows, gate_up_full) for rows in normed_slots]
    hidden_slots = [
        gated_unit(act[:, :ff_cols], act[:, ff_cols:]).astype(BF16) for act in act_slots
    ]
    ffn_out = sum_blocks([matmul_nt(hidden, down_full).astype(BF16) for hidden in hidden_slots])
    mixed_out = (middle + rms_norm(ffn_out, gain_rows[3])).astype(BF16)

    upstream = cotangent.astype(F32)
    grad_ffn, gain_grad_ffn = norm_back(ffn_out, gain_rows[3], upstream)
    grad_slots = both_blocks(grad_ffn.astype(BF16))
    grad_act_slots, grad_second_parts = [], []
    for rows, act in zip(grad_slots, act_slots):
        grad_hidden = matmul(rows, down_full)
        unit_out, unit_back = jax.vjp(gated_unit, act[:, :ff_cols], act[:, ff_cols:])
        grad_act_slots.append(jnp.concatenate(unit_back(grad_hidden), axis=1).astype(BF16))
        grad_second_parts.append(matmul_nt(grad_act_slots[-1], gate_up_full).astype(BF16))
    other = head_reduce(lines, grad_second_parts[1]).astype(BF16)
    other_came = lines.head.came[-1] if size_h > 1 else ()
    other = swap_ctx(lines, other, 1)
    own = head_reduce(lines, after(grad_second_parts[0], *other_came))
    down_rows = after(jnp.concatenate(grad_slots), grad_second_parts[1])
    down_term = matmul_tn(down_rows, jnp.concatenate(hidden_slots)).astype(BF16)
    down_back = units_back(lines, down_term.reshape(size_x * size_z, ff_rows, ff_cols))
    gate_up_rows = after(jnp.concatenate(normed_slots), down_term, *other_came)
    gate_up_term = matmul_tn(gate_up_rows, jnp.concatenate(grad_act_slots))
    gate_up_term = gate_up_term.astype(BF16)
    grad_second = own + other.astype(F32)
    down_other = units_sent(lines, down_back, 1, other)
    down_back = [units_sent(lines, down_back, 0), down_other]
    gate_up_back = units_back(lines, gate_up_term.reshape(size_x * size_z, ff_rows, 2 * ff_cols))
    gate_up_other = units_sent(lines, gate_up_back, 1)

    grad_middle_part, gain_grad_middle = norm_back(middle, gain_rows[2], grad_second)
    grad_middle = upstream + grad_middle_part
    grad_attn, gain_grad_attn = norm_back(attn_out, gain_rows[1], grad_middle)
    block_grad_attn = head_gather(lines, grad_attn.astype(BF16))
    out_term = matmul_tn(attended_low, block_grad_attn).astype(BF16)
    out_term = jnp.transpose(
        out_term.reshape(out_groups, size_h, out_rows, width), (1, 0, 2, 3)
    )
    grad_attended = matmul_nt(block_grad_attn, out_full).astype(BF16)
    grad_attended = heads_of(grad_attended, query_local).astype(F32)
    grad_attended = grad_attended.reshape(kv_local, group * block_rows, HD)
    row_delta = jnp.sum(grad_attended * attended, axis=-1, keepdims=True)
    delta = row_delta / exp_total
    grad_summed = (grad_attended / exp_total).astype(BF16)
    grad_query = 0.0
    kv_parts = {}
    for k in ctx_order():
        query_part, key_part, value_part = block_backward(
            queries, kv_slots[k][0], kv_slots[k][1], query_pos, pos_slots[k], grad_summed, delta
        )
        grad_query = grad_query + query_part
        kv_parts[k] = jnp.stack([key_part, value_part])
    grad_kv = sum_ctx_slots(lines, lambda k: kv_parts[k])
    gate_up_back = [units_sent(lines, gate_up_back, 0), gate_up_other]
    out_sets = head_exchange(lines, pick_pieces(out_term, [own_h ^ i for i in range(size_h)]))
    out_term = place(out_sets, [own_h ^ i for i in range(size_h)])

    grad_query = grad_query.astype(BF16).astype(F32).reshape(query_local, block_rows, HD)
    query_proj = rows_of(rope_back(grad_query, cosine, sine_table) * query_scale).astype(BF16)
    grad_kv = grad_kv.astype(BF16).astype(F32)
    kv_proj = jnp.concatenate(
        [rows_of(rope_back(grad_kv[0], cosine, sine_table)), rows_of(grad_kv[1])], axis=1
    ).astype(BF16)
    grad_proj = jnp.concatenate([query_proj, kv_proj], axis=1)
    qkv_term = matmul_tn(first_normed, grad_proj).astype(BF16)
    qkv_sums = sum_over_fsdp(
        lines, qkv_term.reshape(size_x * size_z, size_h * qkv_rows, local_cols), ctx_order()
    )
    qkv_sum = sum_ctx_slots(lines, lambda k: qkv_sums[k])
    grad_first = head_reduce(lines, matmul_nt(grad_proj, qkv_full).astype(BF16))
    grad_input_part, gain_grad_input = norm_back(inputs, gain_rows[0], grad_first)
    tokens_grad = (grad_middle + grad_input_part).astype(BF16)

    qkv_pieces = head_exchange(lines, split_rows([qkv_sum], own_h))
    out_sums = sum_over_fsdp(
        lines, out_term.reshape(size_x * size_z, out_rows, width), ctx_order()
    )
    out_grad = sum_ctx_slots(lines, lambda k: out_sums[k])
    gains_grad = scatter_gains(
        jnp.stack([gain_grad_input, gain_grad_attn, gain_grad_middle, gain_grad_ffn])
    )

    qkv_grad, qkv_first_new, qkv_second_new, qkv_new = adam_qkv(
        [one[:, :query_cols] for one in qkv_pieces],
        [one[:, query_cols:] for one in qkv_pieces],
        own_h, qkv_weight, qkv_first, qkv_second
    )
    out_first_new, out_second_new, out_new = adam_step(
        out_weight, out_first, out_second, out_grad, RATE_MATRIX, WEIGHT_DECAY
    )
    gate_up_grad, gate_up_first_new, gate_up_second_new, gate_up_new = adam_units(
        gate_up_back, low, gate_up, gate_up_first, gate_up_second, RATE_MATRIX
    )
    down_outs = adam_units(
        down_back,
        low,
        down_turned,
        down_first.T[None],
        down_second.T[None],
        RATE_DOWN,
    )
    down_grad, down_first_new, down_second_new, down_new = [one[0].T for one in down_outs]
    gains_first_new, gains_second_new, gains_new = adam_step(
        gains, gains_first, gains_second, gains_grad, RATE_GAIN, 0.0
    )
    return (
        mixed_out,
        tokens_grad,
        qkv_grad,
        qkv_first_new,
        qkv_second_new,
        qkv_new,
        out_grad,
        out_first_new,
        out_second_new,
        out_new,
        gate_up_grad,
        gate_up_first_new,
        gate_up_second_new,
        gate_up_new,
        down_grad,
        down_first_new,
        down_second_new,
        down_new,
        gains_grad,
        gains_first_new,
        gains_second_new,
        gains_new,
    )


TOKEN_SPEC = P(("fsdp", "ctx", "head"), None)
GATE_UP_SPEC = P(None, ("fsdp", "ctx"), "head")
DOWN_SPEC = P("head", ("fsdp", "ctx"))


def solution(mesh):
    in_specs = (
        (TOKEN_SPEC, P("fsdp"))
        + (TOKEN_SPEC,) * 7
        + (GATE_UP_SPEC,) * 3
        + (DOWN_SPEC,) * 3
        + (TOKEN_SPEC,) * 3
    )
    out_specs = (
        (TOKEN_SPEC,) * 10 + (GATE_UP_SPEC,) * 4 + (DOWN_SPEC,) * 4 + (TOKEN_SPEC,) * 4
    )
    return jax.shard_map(shards, mesh=mesh, in_specs=in_specs, out_specs=out_specs, check_vma=False)
```
